128 devices in a mesh: subj: 8 (over z, x_lo), vox: 16 (over y, x_hi, core).
Axes of the slice: x: 4 (x_hi: 2, x_lo: 2; x = x_hi * 2 + x_lo), y: 4, z: 4, core: 2. Of those that a mesh axis runs over, the one named last changes fastest.
Arguments:
- features: bfloat16 [16384, 4096], P(('subj', 'vox')), may hold values from -20 to 20
- token_ticks: int32 [16384], replicated, may hold values from 0 to 98303, as said below
- offsets: int32 [8], P('subj'), may hold values from 0 to 63
- run_lengths: int32 [8, 8], P('subj'), may hold values from 1 to 512, 1536 in all within a row
- penalty: float32 [8], P('subj'), may hold values from 0.05 to 0.5
- responses: float32 [8, 1536, 2048], P('subj', None, 'vox'), may hold values from -6 to 6
Outputs:
- weights: bfloat16 [8, 4, 4096, 2048], P('subj', None, 'vox')
The draws below stay inside these ranges and needn't reach their ends.
Inputs may be any that keep to these rules, and one draw needn't show every extreme that they name: `token_ticks`: token k's tick lies between k * 6 and k * 6 + 5. `run_lengths`: each subject's 8 runs together cover its 1536 TRs in order.
All inputs are finite; a program needn't handle non-finite values.
Results may differ from the reference program's by a relative error of at most 0.023.
The reference program's roundings to bfloat16 on the way count: a program that leaves them out, or rounds other values in their place, can miss the bound.
Values may be sent and summed in bfloat16 or wider, within the bound.
No kernel may reach another device: no remote copies, remote signals or barrier semaphores. Data moves between devices by JAX's collectives and lax.ppermute only.
A program may use at most 128 MiB of HBM per device.

```python
import math
import jax
import jax.numpy as jnp
import numpy as np
from jax import lax

F = 4096
DELAYS = 4
TICKS = 64
GAP = 6
RUNS = 8
SUBJECTS = 8
TOKENS = 16384
TR_ALL = 1536
VOXELS = 2048


def draw_features(key, part):
    key = jax.random.fold_in(key, 11)
    first_key, second_key, third_key, fourth_key, fifth_key, sixth_key = jax.random.split(key, 6)
    latent_rank = 256
    block_tokens = 8
    amplitude = np.floor(2048.0 * 10.0 ** (-3.0 * np.arange(latent_rank) / latent_rank))
    latent_norm = float(np.sqrt(np.sum(amplitude * amplitude) * (15.0 * 15.0 - 1.0) / 12.0))
    block_count = (TOKENS + block_tokens - 1) // block_tokens
    levels = jax.random.randint(first_key, (block_count, latent_rank), -7, 8, jnp.int32).astype(jnp.float32)
    levels = levels * jnp.asarray(amplitude, jnp.float32)[None, :]
    signs = (jax.random.randint(second_key, (latent_rank, F), 0, 2, jnp.int32) * 2 - 1).astype(jnp.float32)
    latent = jnp.dot(levels, signs, precision=lax.Precision.HIGHEST)
    latent = jnp.repeat(latent, block_tokens, axis=0)[:TOKENS] / latent_norm
    column_scale = jnp.exp(jax.random.uniform(third_key, (1, F), jnp.float32) * math.log(10.0)) / 4.64
    row_scale = jnp.exp(jax.random.uniform(fourth_key, (TOKENS, 1), jnp.float32) * math.log(10.0)) / 4.64
    noise = jnp.clip(jax.random.normal(fifth_key, (TOKENS, F), jnp.float32), -4.0, 4.0) * 0.85
    shared_part = jnp.clip(jax.random.normal(sixth_key, (1, F), jnp.float32) * 0.3, -1.0, 1.0)
    values = latent * 1.6 + noise + shared_part
    return jnp.clip(values * row_scale * column_scale, -20.0, 20.0).astype(jnp.bfloat16)


def draw_token_ticks(key, part):
    key = jax.random.fold_in(key, 5)
    jitter = jax.random.randint(key, (TOKENS,), 0, GAP, jnp.int32)
    jitter = jitter.at[0].set(0).at[TOKENS - 1].set(GAP - 1)
    return jnp.arange(TOKENS, dtype=jnp.int32) * GAP + jitter


def plant(entries, stream_key, least, high):
    longest = entries.shape.index(max(entries.shape))
    spots = []
    for shift in (0, 1):
        where = [jax.random.randint(jax.random.fold_in(stream_key, axis), (), 0, length) for axis, length in enumerate(entries.shape)]
        where[longest] = (where[longest] + shift) % entries.shape[longest]
        spots.append(tuple(where))
    return entries.at[spots[0]].set(least).at[spots[1]].set(high)


def level_of(own_key, dims, shards, least, top_value):
    def one(position, parts):
        heights = jax.random.uniform(jax.random.fold_in(jax.random.fold_in(own_key, 6), position), (parts,), jnp.float32, least / len(shards), top_value / len(shards))
        return jnp.repeat(jnp.exp(heights), dims[position] // parts).reshape((-1,) + (1,) * (len(dims) - position - 1))

    level = one(*shards[0])
    for cut in shards[1:]:
        level = level * one(*cut)
    return level


def length_profile(number_of, total, most, skew):
    weights = [(1 << 20) // math.isqrt(rank ** skew) + 1 for rank in range(2, number_of + 1)]
    surplus, holding = total - most - (number_of - 1), [1] * (number_of - 1)
    while surplus > 0:
        free = [i for i in range(number_of - 1) if holding[i] < most]
        whole, left = sum([weights[i] for i in free]), surplus
        for i in free:
            addition = min(most - holding[i], max(1, left * weights[i] // whole), surplus)
            holding[i] = holding[i] + addition
            surplus = surplus - addition
    return np.array([most] + holding)


def ragged(stream_key, count, total, bound, slope):
    if count == 2:
        one = jax.random.randint(stream_key, (), max(1, total - bound), min(bound, total - 1) + 1)
        return jnp.stack([one, total - one])
    tallies = jnp.asarray(length_profile(count, total, bound, slope), jnp.int32)
    pairs = (count - 1) // 2
    giver, taker = tallies[1:1 + 2 * pairs:2], tallies[2:2 + 2 * pairs:2]
    slack = jnp.minimum(giver - 1, bound - taker)
    passed = jax.random.randint(jax.random.fold_in(stream_key, 1), (pairs,), 0, 1 << 20) % (slack + 1)
    tallies = tallies.at[1:1 + 2 * pairs:2].set(giver - passed).at[2:2 + 2 * pairs:2].set(taker + passed)
    return tallies[jax.random.permutation(jax.random.fold_in(stream_key, 2), count)]


def bell_draw(key, dims, scale, limit, cuts=(), held_as=jnp.bfloat16):
    result = scale * jax.random.normal(key, dims, jnp.float32)
    if cuts:
        result = result * level_of(key, dims, cuts, -0.22, 0.18)
    return jnp.clip(result, -limit, limit).astype(held_as)


def setup_inputs(seed: int = 0) -> dict:
    key_list = jax.random.split(jax.random.key(seed), 7)
    features = draw_features(jax.random.fold_in(key_list[6], 71), 0)
    token_ticks = draw_token_ticks(jax.random.fold_in(key_list[6], 71), 0)
    offsets = plant(jax.random.randint(key_list[2], (SUBJECTS,), 0, TICKS), jax.random.fold_in(key_list[2], 1), 0, TICKS - 1).astype(jnp.int32)
    run_lengths = jax.vmap(lambda own: ragged(own, RUNS, TR_ALL, TR_ALL // 3, 1))(jax.random.split(key_list[3], SUBJECTS)).reshape((SUBJECTS, RUNS)).astype(jnp.int32)
    penalty = jnp.clip(jnp.exp(math.log(0.5) - 2.3025851 * jax.random.uniform(key_list[4], (SUBJECTS,), jnp.float32) ** level_of(key_list[4], (SUBJECTS,), ((0, 8),), -0.2, 0.2)), 0.05, 0.5)
    responses = bell_draw(key_list[5], (SUBJECTS, TR_ALL, VOXELS), 1.0, 6.0, ((0, 8), (2, 16)), jnp.float32)
    return dict(features=features, token_ticks=token_ticks, offsets=offsets, run_lengths=run_lengths, penalty=penalty, responses=responses)


def lanczos_table(token_ticks, offset, tr_rows):
    distance = token_ticks[None, :] - (tr_rows[:, None] * TICKS + offset)
    inside = jnp.abs(distance) < 3 * TICKS
    scaled = distance.astype(jnp.float32) / TICKS
    shaped = jnp.sinc(scaled) * jnp.sinc(scaled / 3.0)
    return jnp.where(inside, shaped, jnp.zeros_like(shaped)).astype(jnp.bfloat16)

def delay_stack(interp, lengths, tr_total):
    starts = jnp.cumsum(lengths) - lengths
    tr_steps = jnp.arange(tr_total, dtype=jnp.int32)
    run_first = jnp.max(jnp.where(starts[None, :] <= tr_steps[:, None], starts[None, :], 0), axis=1)
    delayed = []
    for delay_step in range(1, DELAYS + 1):
        moved = jnp.concatenate([jnp.zeros((delay_step, interp.shape[1]), interp.dtype), interp[:-delay_step]], axis=0)
        keep_rows = (tr_steps - delay_step >= run_first)[:, None]
        delayed.append(jnp.where(keep_rows, moved, jnp.zeros_like(moved)))
    return jnp.stack(delayed, axis=1)

def reference(features, token_ticks, offsets, run_lengths, penalty, responses):
    features_wide = features.astype(jnp.float32)
    tr_rows = jnp.arange(TR_ALL, dtype=jnp.int32)
    spread = (GAP / TICKS) ** 0.5

    def one_subject(inputs):
        offset, lengths, ridge, targets = inputs
        weights_table = lanczos_table(token_ticks, offset, tr_rows).astype(jnp.float32)
        summed = jnp.dot(weights_table, features_wide, precision=lax.Precision.HIGHEST)
        interp = (summed * spread).astype(jnp.bfloat16)
        stacked = delay_stack(interp, lengths, TR_ALL).reshape(TR_ALL, DELAYS * F).astype(jnp.float32)
        kernel = jnp.dot(stacked, stacked.T, precision=lax.Precision.HIGHEST) / (DELAYS * F)
        system = kernel + ridge * jnp.eye(TR_ALL, dtype=jnp.float32)
        factor = jnp.linalg.cholesky(system)
        forward = lax.linalg.triangular_solve(factor, targets, left_side=True, lower=True)
        dual_coef = lax.linalg.triangular_solve(factor, forward, left_side=True, lower=True, transpose_a=True).astype(jnp.bfloat16)
        projected = jnp.dot(stacked.T, dual_coef.astype(jnp.float32), precision=lax.Precision.HIGHEST)
        projected = projected * (DELAYS * F) ** (-0.5)
        return projected.reshape(DELAYS, F, VOXELS).astype(jnp.bfloat16)
    return lax.map(one_subject, (offsets, run_lengths, penalty, responses))
```

```python
import jax
import jax.numpy as jnp
from jax import lax
from jax.experimental import pallas as pl
from jax.experimental.pallas import tpu as pltpu
from jax.sharding import PartitionSpec as P

DELAYS = 4
TICKS = 64
GAP = 6
F = 4096
SUBJ = 8
VOX = 16
N = 1536
SLAB = F // VOX
COLS = 128
W = 256
PANELS = N // W
EDGE = 16
HALO = 32
STEP = 24
HI = lax.Precision.HIGHEST
NT = (((1,), (1,)), ((), ()))


def mm(a, b):
    return jnp.dot(a, b, precision=HI, preferred_element_type=jnp.float32)


def mmt(a, b):
    return lax.dot_general(a, b, NT, precision=HI, preferred_element_type=jnp.float32)


def tri_inverse(block):
    rows = [block[8 * g : 8 * g + 8, :] for g in range(16)]
    shape = (8, 128)
    lane = lax.broadcasted_iota(jnp.int32, shape, 1)
    sub = lax.broadcasted_iota(jnp.int32, shape, 0)
    for g in range(16):
        base = 8 * g
        here = rows[g]
        col = [jnp.broadcast_to(here[:, base + m : base + m + 1], shape) for m in range(8)]
        a = [[jnp.broadcast_to(col[m][j : j + 1, :], shape) for m in range(j + 1)] for j in range(8)]
        x = [[None] * 8 for _ in range(8)]
        for p in range(8):
            inv = lax.rsqrt(a[p][p])
            for j in range(p):
                x[p][j] = x[p][j] * inv
            x[p][p] = inv
            low = {i: a[i][p] * inv for i in range(p + 1, 8)}
            for i in range(p + 1, 8):
                for j in range(p + 1, i + 1):
                    a[i][j] = a[i][j] - low[i] * low[j]
                for j in range(p + 1):
                    term = low[i] * x[p][j]
                    x[i][j] = -term if x[i][j] is None else x[i][j] - term
        inside = (lane >= base) & (lane < base + 8)
        unit = jnp.where(inside, jnp.where(lane - base == sub, 1.0, 0.0), here)
        r = [jnp.broadcast_to(unit[m : m + 1, :], shape) for m in range(8)]
        hat = []
        for q in range(8):
            acc = x[q][0] * r[0]
            for m in range(1, q + 1):
                acc = acc + x[q][m] * r[m]
            hat.append(acc)
        out = hat[0]
        for q in range(1, 8):
            out = jnp.where(sub == q, hat[q], out)
        rows[g] = jnp.where(lane < base + 8, out, 0.0)
        if g < 15:
            full = []
            for m in range(8):
                acc = x[7][m] * hat[7]
                for q in range(6, m - 1, -1):
                    acc = acc + x[q][m] * hat[q]
                full.append(acc)
            for i in range(g + 1, 16):
                old = rows[i]
                acc = jnp.where(inside, 0.0, old)
                for m in range(8):
                    acc = acc - jnp.broadcast_to(old[:, base + m : base + m + 1], shape) * full[m]
                rows[i] = acc
    return jnp.concatenate(rows, axis=0)


def cut(i, size=W):
    return pl.ds(pl.multiple_of(i * size, size), size)


def solve_kernel(pen_ref, all_ref, b_ref, pr_ref, pc_ref, o_ref, xs_ref, a_ref, strip_ref, inv_ref, sem):
    tail = pl.ds(N, COLS)
    copies = [
        pltpu.make_async_copy(all_ref.at[v], xs_ref.at[pl.ds(EDGE, N), pl.ds(v * SLAB, SLAB)], sem.at[v])
        for v in range(VOX)
    ]
    copies.append(pltpu.make_async_copy(b_ref, a_ref.at[tail, :], sem.at[VOX]))
    for c in copies:
        c.start()
    xs_ref[0:EDGE, :] = jnp.zeros((EDGE, F), jnp.bfloat16)
    strip_ref[:, 0:128] = jnp.zeros((W + EDGE, 128), jnp.float32)
    for c in copies:
        c.wait()
    pen = pen_ref[0]
    scale = 1.0 / (DELAYS * F)

    def gram(i, _):
        left = xs_ref[pl.ds(pl.multiple_of(i * W, W), W + EDGE), :]

        def one(j, _):
            right = xs_ref[pl.ds(pl.multiple_of(j * W + EDGE, EDGE), W), :]
            strip_ref[:, pl.ds(pl.multiple_of(j * W + 128, 128), W)] = lax.dot_general(
                left, right, NT, preferred_element_type=jnp.float32
            )
            return 0

        lax.fori_loop(0, i + 1, one, 0)
        row_pos = pr_ref[cut(i), :]

        def shift(j, _):
            t = strip_ref[:, pl.ds(pl.multiple_of(j * W, 128), W + 128)]
            near = jnp.minimum(row_pos, pc_ref[0:1, cut(j)])
            total = jnp.zeros((W, W), jnp.float32)
            for k in range(1, DELAYS + 1):
                t = pltpu.roll(pltpu.roll(t, 1, 0), 1, 1)
                total = total + jnp.where(near >= k, t[EDGE:, 128:], 0.0)
            total = total * scale
            row = lax.broadcasted_iota(jnp.int32, (W, W), 0) + i * W
            colm = lax.broadcasted_iota(jnp.int32, (W, W), 1) + j * W
            a_ref[cut(i), cut(j)] = jnp.where(row == colm, total + pen, total)
            return 0

        lax.fori_loop(0, i + 1, shift, 0)
        return 0

    lax.fori_loop(0, PANELS, gram, 0)

    def panel(p, _):
        def half(h, _):
            d = 2 * p + h
            blk = cut(d, 128)
            inv_ref[p, cut(h, 128), cut(h, 128)] = tri_inverse(a_ref[blk, blk])

            @pl.when(h == 0)
            def _():
                below = cut(d + 1, 128)
                c = mmt(a_ref[below, blk], inv_ref[p, 0:128, 0:128])
                a_ref[below, blk] = c
                a_ref[below, below] -= mmt(c, c)

            return 0

        lax.fori_loop(0, 2, half, 0)
        low = a_ref[cut(2 * p + 1, 128), cut(2 * p, 128)]
        inv_ref[p, 128:256, 0:128] = -mm(inv_ref[p, 128:256, 128:256], mm(low, inv_ref[p, 0:128, 0:128]))
        inv_ref[p, 0:128, 128:256] = jnp.zeros((128, 128), jnp.float32)
        here = cut(p)

        def scale_rows(i, _):
            a_ref[cut(i), here] = mmt(a_ref[cut(i), here], inv_ref[p])
            return 0

        lax.fori_loop(p + 1, PANELS, scale_rows, 0)
        a_ref[tail, here] = mmt(a_ref[tail, here], inv_ref[p])

        def column(j, _):
            right = a_ref[cut(j), here]

            def update(i, _):
                a_ref[cut(i), cut(j)] -= mmt(a_ref[cut(i), here], right)
                return 0

            lax.fori_loop(j, PANELS, update, 0)
            a_ref[tail, cut(j)] -= mmt(a_ref[tail, here], right)
            return 0

        lax.fori_loop(p + 1, PANELS, column, 0)
        return 0

    lax.fori_loop(0, PANELS, panel, 0)

    def back(q, _):
        p = PANELS - 1 - q
        x = mm(a_ref[tail, cut(p)], inv_ref[p])
        a_ref[tail, cut(p)] = x

        def push(j, _):
            a_ref[tail, cut(j)] -= mm(x, a_ref[cut(p), cut(j)])
            return 0

        lax.fori_loop(0, p, push, 0)
        return 0

    lax.fori_loop(0, PANELS, back, 0)
    o_ref[...] = a_ref[tail, :].astype(o_ref.dtype)


def solve_call(pen, gathered, targets, row_pos, col_pos):
    anywhere = pl.BlockSpec(memory_space=pl.ANY)
    vmem = pl.BlockSpec(memory_space=pltpu.VMEM)
    return pl.pallas_call(
        solve_kernel,
        out_shape=jax.ShapeDtypeStruct((COLS, N), jnp.bfloat16),
        in_specs=[pl.BlockSpec(memory_space=pltpu.SMEM), anywhere, anywhere, vmem, vmem],
        out_specs=vmem,
        scratch_shapes=[
            pltpu.VMEM((N + EDGE, F), jnp.bfloat16),
            pltpu.VMEM((N + COLS, N), jnp.float32),
            pltpu.VMEM((W + EDGE, N + 128), jnp.float32),
            pltpu.VMEM((PANELS, W, W), jnp.float32),
            pltpu.SemaphoreType.DMA((VOX + 1,)),
        ],
        compiler_params=pltpu.CompilerParams(vmem_limit_bytes=52 * 2**20),
        cost_estimate=pl.CostEstimate(flops=3 * 10**10, bytes_accessed=2 * 10**7, transcendentals=0),
    )(pen, gathered, targets, row_pos, col_pos)


def lanczos(ticks, centers):
    distance = ticks[None, :] - centers[:, None]
    inside = jnp.abs(distance) < 3 * TICKS
    scaled = distance.astype(jnp.float32) / TICKS
    shaped = jnp.sinc(scaled) * jnp.sinc(scaled / 3.0)
    return jnp.where(inside, shaped, jnp.zeros_like(shaped)).astype(jnp.bfloat16)


def all_offsets(offsets):
    mine = lax.axis_index("subj")
    wide = jnp.broadcast_to(offsets, (8, 128))
    got = [wide]
    for hop in range(1, SUBJ):
        got.append(lax.ppermute(wide, "subj", [(i, (i - hop) % SUBJ) for i in range(SUBJ)]))
    stacked = jnp.stack([g[0, 0] for g in got])
    return jnp.roll(stacked, mine)


def body(features, token_ticks, offsets, run_lengths, penalty, responses):
    group = lax.axis_index("subj")
    rows = N // SUBJ
    tokens = token_ticks.shape[0] // SUBJ
    every = all_offsets(offsets)
    columns = lax.all_to_all(features, "vox", split_axis=1, concat_axis=0, tiled=True)
    before = lax.ppermute(columns[-HALO:], "subj", [(i, i + 1) for i in range(SUBJ - 1)])
    after = lax.ppermute(columns[:HALO], "subj", [(i + 1, i) for i in range(SUBJ - 1)])
    ext = jnp.concatenate([before, columns, after], axis=0)
    far = jnp.full((HALO,), -(2**20), jnp.int32)
    near_ticks = lax.dynamic_slice_in_dim(
        jnp.concatenate([far, token_ticks, far]), group * tokens, tokens + 2 * HALO, 0
    )
    spread = (GAP / TICKS) ** 0.5
    span = STEP * TICKS // GAP
    steps = jnp.arange(STEP, dtype=jnp.int32)
    pieces = []
    for b in range(rows // STEP):
        first = group * rows + b * STEP
        centers = ((first + steps)[None, :] * TICKS + every[:, None]).reshape(-1)
        low = b * span
        table = lanczos(near_ticks[low : low + span + 2 * HALO], centers)
        summed = jnp.dot(table, ext[low : low + span + 2 * HALO], preferred_element_type=jnp.float32)
        pieces.append((summed * spread).astype(jnp.bfloat16).reshape(SUBJ, STEP, SLAB))
    local = jnp.stack(pieces, axis=1).reshape(SUBJ * rows, SLAB)
    interp = lax.all_to_all(local, "subj", split_axis=0, concat_axis=0, tiled=True)
    gathered = lax.all_gather(interp, "vox", axis=0, tiled=False)

    lengths = run_lengths[0]
    starts = jnp.cumsum(lengths) - lengths
    tr_steps = jnp.arange(N, dtype=jnp.int32)
    run_first = jnp.max(jnp.where(starts[None, :] <= tr_steps[:, None], starts[None, :], 0), axis=1)
    pos = tr_steps - run_first
    dual = solve_call(
        penalty,
        gathered,
        responses[0].T,
        pos[:, None],
        jnp.broadcast_to(pos[None, :], (8, N)),
    )
    delayed = []
    for k in range(1, DELAYS + 1):
        moved = jnp.concatenate([jnp.zeros((k, SLAB), interp.dtype), interp[:-k]], axis=0)
        delayed.append(jnp.where((pos >= k)[:, None], moved, jnp.zeros_like(moved)))
    stacked = jnp.concatenate(delayed, axis=1)
    projected = lax.dot_general(
        stacked,
        lax.all_gather(dual, "vox", axis=0, tiled=True),
        (((0,), (1,)), ((), ())),
        preferred_element_type=jnp.float32,
    )
    projected = (projected * (DELAYS * F) ** (-0.5)).astype(jnp.bfloat16)
    return projected.reshape(1, DELAYS, SLAB, projected.shape[1])


def solution(mesh):
    return jax.shard_map(
        body,
        mesh=mesh,
        in_specs=(
            P(("subj", "vox"), None),
            P(),
            P("subj"),
            P("subj", None),
            P("subj"),
            P("subj", None, "vox"),
        ),
        out_specs=P("subj", None, "vox", None),
        check_vma=False,
    )
```

```python
import jax
import jax.numpy as jnp
from jax import lax
from jax.experimental import pallas as pl
from jax.experimental.pallas import tpu as pltpu
from jax.sharding import PartitionSpec as P

DELAYS = 4
TICKS = 64
GAP = 6
F = 4096
SUBJ = 8
VOX = 16
N = 1536
SLAB = F // VOX
COLS = 128
W = 256
PANELS = N // W
EDGE = 16
HALO = 32
VMEM_LIMIT = 52 * 2**20
STEP = 24
HALF = F // 2
CHIPS = 8
PART = N // 2
CUTP = PANELS // 2
HI = lax.Precision.HIGHEST
NT = (((1,), (1,)), ((), ()))


def mm(a, b):
    return jnp.dot(a, b, precision=HI, preferred_element_type=jnp.float32)


def mmt(a, b):
    return lax.dot_general(a, b, NT, precision=HI, preferred_element_type=jnp.float32)


def tri_inverse(block):
    rows = [block[8 * g : 8 * g + 8, :] for g in range(16)]
    shape = (8, 128)
    lane = lax.broadcasted_iota(jnp.int32, shape, 1)
    sub = lax.broadcasted_iota(jnp.int32, shape, 0)
    for g in range(16):
        base = 8 * g
        here = rows[g]
        col = [jnp.broadcast_to(here[:, base + m : base + m + 1], shape) for m in range(8)]
        a = [[jnp.broadcast_to(col[m][j : j + 1, :], shape) for m in range(j + 1)] for j in range(8)]
        x = [[None] * 8 for _ in range(8)]
        for p in range(8):
            inv = lax.rsqrt(a[p][p])
            for j in range(p):
                x[p][j] = x[p][j] * inv
            x[p][p] = inv
            low = {i: a[i][p] * inv for i in range(p + 1, 8)}
            for i in range(p + 1, 8):
                for j in range(p + 1, i + 1):
                    a[i][j] = a[i][j] - low[i] * low[j]
                for j in range(p + 1):
                    term = low[i] * x[p][j]
                    x[i][j] = -term if x[i][j] is None else x[i][j] - term
        inside = (lane >= base) & (lane < base + 8)
        unit = jnp.where(inside, jnp.where(lane - base == sub, 1.0, 0.0), here)
        r = [jnp.broadcast_to(unit[m : m + 1, :], shape) for m in range(8)]
        hat = []
        for q in range(8):
            acc = x[q][0] * r[0]
            for m in range(1, q + 1):
                acc = acc + x[q][m] * r[m]
            hat.append(acc)
        out = hat[0]
        for q in range(1, 8):
            out = jnp.where(sub == q, hat[q], out)
        rows[g] = jnp.where(lane < base + 8, out, 0.0)
        if g < 15:
            full = []
            for m in range(8):
                acc = x[7][m] * hat[7]
                for q in range(6, m - 1, -1):
                    acc = acc + x[q][m] * hat[q]
                full.append(acc)
            for i in range(g + 1, 16):
                old = rows[i]
                acc = jnp.where(inside, 0.0, old)
                for m in range(8):
                    acc = acc - jnp.broadcast_to(old[:, base + m : base + m + 1], shape) * full[m]
                rows[i] = acc
    return jnp.concatenate(rows, axis=0)


def cut(i, size=W):
    return pl.ds(pl.multiple_of(i * size, size), size)


def assemble(raw_ref, xs_ref, first):
    for g in range(SUBJ // 2):
        low = STEP * g // 16 * 16
        off = STEP * g - low

        def one(u, _, g=g, low=low, off=off):
            dest = pl.ds(pl.multiple_of(first + 192 * g + 48 * u, 16), 48)
            for c in range(2):
                pair = [
                    raw_ref[4 * u + 2 * e + c, low : low + 32, :].astype(jnp.float32)[off : off + STEP]
                    for e in range(2)
                ]
                xs_ref[dest, c * HALF : (c + 1) * HALF] = jnp.concatenate(pair, axis=0).astype(jnp.bfloat16)
            return 0

        lax.fori_loop(0, CHIPS // 2, one, 0)


def gram_rows(first, last, pen, xs_ref, a_ref, strip_ref, pr_ref, pc_ref):
    scale = 1.0 / (DELAYS * F)

    def gram(i, _):
        left = xs_ref[pl.ds(pl.multiple_of(i * W, W), W + EDGE), :]

        def one(j, _):
            right = xs_ref[pl.ds(pl.multiple_of(j * W + EDGE, EDGE), W), :]
            strip_ref[:, pl.ds(pl.multiple_of(j * W + 128, 128), W)] = lax.dot_general(
                left, right, NT, preferred_element_type=jnp.float32
            )
            return 0

        lax.fori_loop(0, i + 1, one, 0)
        row_pos = pr_ref[cut(i), :]

        def shift(j, _):
            t = strip_ref[:, pl.ds(pl.multiple_of(j * W, 128), W + 128)]
            near = jnp.minimum(row_pos, pc_ref[0:1, cut(j)])
            total = jnp.zeros((W, W), jnp.float32)
            for k in range(1, DELAYS + 1):
                t = pltpu.roll(pltpu.roll(t, 1, 0), 1, 1)
                total = total + jnp.where(near >= k, t[EDGE:, 128:], 0.0)
            total = total * scale
            row = lax.broadcasted_iota(jnp.int32, (W, W), 0) + i * W
            column = lax.broadcasted_iota(jnp.int32, (W, W), 1) + j * W
            a_ref[cut(i), cut(j)] = jnp.where(row == column, total + pen, total)
            return 0

        lax.fori_loop(0, i + 1, shift, 0)
        return 0

    lax.fori_loop(first, last, gram, 0)


def diagonal(p, a_ref, inv_ref):
    def half(h, _):
        d = 2 * p + h
        blk = cut(d, 128)
        inv_ref[p, cut(h, 128), cut(h, 128)] = tri_inverse(a_ref[blk, blk])

        @pl.when(h == 0)
        def _():
            below = cut(d + 1, 128)
            c = mmt(a_ref[below, blk], inv_ref[p, 0:128, 0:128])
            a_ref[below, blk] = c
            a_ref[below, below] -= mmt(c, c)

        return 0

    lax.fori_loop(0, 2, half, 0)
    low = a_ref[cut(2 * p + 1, 128), cut(2 * p, 128)]
    inv_ref[p, 128:256, 0:128] = -mm(inv_ref[p, 128:256, 128:256], mm(low, inv_ref[p, 0:128, 0:128]))
    inv_ref[p, 0:128, 128:256] = jnp.zeros((128, 128), jnp.float32)


def eliminate(p, first, last, a_ref, inv_ref):
    here = cut(p)

    def scale_rows(i, _):
        a_ref[cut(i), here] = mmt(a_ref[cut(i), here], inv_ref[p])
        return 0

    lax.fori_loop(first, last, scale_rows, 0)

    def column(j, _):
        right = a_ref[cut(j), here]

        def update(i, _):
            a_ref[cut(i), cut(j)] -= mmt(a_ref[cut(i), here], right)
            return 0

        lax.fori_loop(jnp.maximum(j, first), last, update, 0)
        return 0

    lax.fori_loop(p + 1, last, column, 0)


def forward(p, first, last, a_ref, inv_ref, tail_ref):
    here = cut(p)

    def update(j, _):
        tail_ref[:, cut(j)] -= mmt(tail_ref[:, here], a_ref[cut(j), here])
        return 0

    lax.fori_loop(first, last, update, 0)


def first_kernel(*refs):
    (where_ref, pen_ref), refs = refs[:2], refs[2:]
    pieces, refs = refs[:PIECES], refs[PIECES:]
    b_ref, pr_ref, pc_ref, rows_out, low_out, inv_out, tail_out, slab_out = refs[:8]
    raw_ref, xs_ref, a_ref, strip_ref, inv_ref, tail_ref, sem = refs[8:]
    copies = []
    for n, (key, start, size) in enumerate(PIECE_LIST):
        copies.append(
            pltpu.make_async_copy(pieces[n], raw_ref.at[where_ref[key], pl.ds(start, size), :], sem.at[n])
        )
    copies.append(pltpu.make_async_copy(b_ref, tail_ref, sem.at[PIECES]))
    for c in copies:
        c.start()
    xs_ref[0:EDGE, :] = jnp.zeros((EDGE, F), jnp.bfloat16)
    strip_ref[:, 0:128] = jnp.zeros((W + EDGE, 128), jnp.float32)
    for c in copies:
        c.wait()
    assemble(raw_ref, xs_ref, EDGE)
    own = pl.ds(EDGE, PART)
    mine = pl.ds(pl.multiple_of(where_ref[0] * SLAB, SLAB), SLAB)
    outs = [
        pltpu.make_async_copy(xs_ref.at[own, :], rows_out, sem.at[PIECES + 1]),
        pltpu.make_async_copy(xs_ref.at[own, mine], slab_out, sem.at[PIECES + 2]),
    ]
    for c in outs:
        c.start()
    gram_rows(0, CUTP, pen_ref[0], xs_ref, a_ref, strip_ref, pr_ref, pc_ref)

    def panel(p, _):
        diagonal(p, a_ref, inv_ref)
        eliminate(p, p + 1, CUTP, a_ref, inv_ref)
        tail_ref[:, cut(p)] = mmt(tail_ref[:, cut(p)], inv_ref[p])
        forward(p, p + 1, CUTP, a_ref, inv_ref, tail_ref)
        return 0

    lax.fori_loop(0, CUTP, panel, 0)
    more = [
        pltpu.make_async_copy(a_ref, low_out, sem.at[PIECES + 3]),
        pltpu.make_async_copy(inv_ref, inv_out, sem.at[PIECES + 4]),
        pltpu.make_async_copy(tail_ref, tail_out, sem.at[PIECES + 5]),
    ]
    for c in more:
        c.start()
    for c in outs + more:
        c.wait()


def second_kernel(
    where_ref, pen_ref, all_ref, rows_in, low_in, inv_in, tail_in, pr_ref, pc_ref, o_ref, slab_out,
    raw_ref, xs_ref, a_ref, strip_ref, inv_ref, tail_ref, sem,
):
    chunk = pltpu.make_async_copy(all_ref, raw_ref, sem.at[0])
    copies = [
        pltpu.make_async_copy(rows_in, xs_ref.at[pl.ds(EDGE, PART), :], sem.at[1]),
        pltpu.make_async_copy(low_in, a_ref.at[pl.ds(0, PART), pl.ds(0, PART)], sem.at[2]),
        pltpu.make_async_copy(inv_in, inv_ref.at[pl.ds(0, CUTP)], sem.at[3]),
        pltpu.make_async_copy(tail_in, tail_ref, sem.at[4]),
    ]
    chunk.start()
    for c in copies:
        c.start()
    strip_ref[:, 0:128] = jnp.zeros((W + EDGE, 128), jnp.float32)
    chunk.wait()
    assemble(raw_ref, xs_ref, EDGE + PART)
    mine = pl.ds(pl.multiple_of(where_ref[0] * SLAB, SLAB), SLAB)
    slab = pltpu.make_async_copy(xs_ref.at[pl.ds(EDGE + PART, PART), mine], slab_out, sem.at[5])
    slab.start()
    for c in copies:
        c.wait()
    gram_rows(CUTP, PANELS, pen_ref[0], xs_ref, a_ref, strip_ref, pr_ref, pc_ref)

    def old(p, _):
        eliminate(p, CUTP, PANELS, a_ref, inv_ref)
        forward(p, CUTP, PANELS, a_ref, inv_ref, tail_ref)
        return 0

    lax.fori_loop(0, CUTP, old, 0)

    def panel(p, _):
        diagonal(p, a_ref, inv_ref)
        eliminate(p, p + 1, PANELS, a_ref, inv_ref)
        tail_ref[:, cut(p)] = mmt(tail_ref[:, cut(p)], inv_ref[p])
        forward(p, p + 1, PANELS, a_ref, inv_ref, tail_ref)
        return 0

    lax.fori_loop(CUTP, PANELS, panel, 0)

    def back(q, _):
        p = PANELS - 1 - q
        x = mm(tail_ref[:, cut(p)], inv_ref[p])
        tail_ref[:, cut(p)] = x

        def push(j, _):
            tail_ref[:, cut(j)] -= mm(x, a_ref[cut(p), cut(j)])
            return 0

        lax.fori_loop(0, p, push, 0)
        return 0

    lax.fori_loop(0, PANELS, back, 0)
    o_ref[...] = tail_ref[...].astype(o_ref.dtype)
    slab.wait()


ANYWHERE = pl.BlockSpec(memory_space=pl.ANY)
IN_VMEM = pl.BlockSpec(memory_space=pltpu.VMEM)
IN_SMEM = pl.BlockSpec(memory_space=pltpu.SMEM)


def scratches(rows, sems):
    return [
        pltpu.VMEM((VOX, STEP * SUBJ // 2, HALF), jnp.bfloat16),
        pltpu.VMEM((rows + EDGE, F), jnp.bfloat16),
        pltpu.VMEM((rows, rows), jnp.float32),
        pltpu.VMEM((W + EDGE, rows + 128), jnp.float32),
        pltpu.VMEM((rows // W, W, W), jnp.float32),
        pltpu.VMEM((COLS, N), jnp.float32),
        pltpu.SemaphoreType.DMA((sems,)),
    ]


def first_call(where, pen, pieces, targets, row_pos, col_pos):
    return pl.pallas_call(
        first_kernel,
        out_shape=[
            jax.ShapeDtypeStruct((PART, F), jnp.bfloat16),
            jax.ShapeDtypeStruct((PART, PART), jnp.float32),
            jax.ShapeDtypeStruct((CUTP, W, W), jnp.float32),
            jax.ShapeDtypeStruct((COLS, N), jnp.float32),
            jax.ShapeDtypeStruct((PART, SLAB), jnp.bfloat16),
        ],
        in_specs=[IN_SMEM, IN_SMEM] + [ANYWHERE] * PIECES + [ANYWHERE, IN_VMEM, IN_VMEM],
        out_specs=[ANYWHERE] * 5,
        scratch_shapes=scratches(PART, PIECES + 6),
        compiler_params=pltpu.CompilerParams(vmem_limit_bytes=VMEM_LIMIT),
        cost_estimate=pl.CostEstimate(flops=3 * 10**10, bytes_accessed=2 * 10**7, transcendentals=0),
    )(where, pen, *pieces, targets, row_pos, col_pos)


def second_call(where, pen, gathered, state, row_pos, col_pos):
    return pl.pallas_call(
        second_kernel,
        out_shape=[
            jax.ShapeDtypeStruct((COLS, N), jnp.bfloat16),
            jax.ShapeDtypeStruct((PART, SLAB), jnp.bfloat16),
        ],
        in_specs=[IN_SMEM, IN_SMEM] + [ANYWHERE] * 5 + [IN_VMEM, IN_VMEM],
        out_specs=[IN_VMEM, ANYWHERE],
        scratch_shapes=scratches(N, 6),
        compiler_params=pltpu.CompilerParams(vmem_limit_bytes=VMEM_LIMIT),
        cost_estimate=pl.CostEstimate(flops=5 * 10**10, bytes_accessed=2 * 10**7, transcendentals=0),
    )(where, pen, gathered, *state, row_pos, col_pos)


def project_kernel(where_ref, st_ref, *refs):
    pieces, out_ref, xt_ref, buf_ref, sem, out_sem = refs[:PIECES], refs[PIECES], *refs[PIECES + 1 :]
    copies = []
    for n, (key, start, size) in enumerate(DUAL_LIST):
        row = pl.multiple_of(where_ref[key] * COLS + start, 16)
        copies.append(pltpu.make_async_copy(pieces[n], xt_ref.at[pl.ds(row, size), :], sem.at[n]))
    for c in copies:
        c.start()
    for c in copies:
        c.wait()
    scale = (DELAYS * F) ** (-0.5)
    sent = []
    for n in range(VOX // 2):
        slot = n % 2
        if n >= 2:
            sent[n - 2].wait()
        got = lax.dot_general(
            st_ref[...], xt_ref[n * W : (n + 1) * W, :], NT, preferred_element_type=jnp.float32
        )
        buf_ref[slot] = (got * scale).astype(jnp.bfloat16)
        sent.append(pltpu.make_async_copy(buf_ref.at[slot], out_ref.at[:, pl.ds(n * W, W)], out_sem.at[slot]))
        sent[n].start()
    for c in sent[-2:]:
        c.wait()


def project_call(where, stacked, pieces):
    return pl.pallas_call(
        project_kernel,
        out_shape=jax.ShapeDtypeStruct((DELAYS * SLAB, VOX * COLS), jnp.bfloat16),
        in_specs=[IN_SMEM, IN_VMEM] + [ANYWHERE] * PIECES,
        out_specs=ANYWHERE,
        scratch_shapes=[
            pltpu.VMEM((VOX * COLS, N), jnp.bfloat16),
            pltpu.VMEM((2, DELAYS * SLAB, W), jnp.bfloat16),
            pltpu.SemaphoreType.DMA((PIECES,)),
            pltpu.SemaphoreType.DMA((2,)),
        ],
        compiler_params=pltpu.CompilerParams(vmem_limit_bytes=VMEM_LIMIT),
        cost_estimate=pl.CostEstimate(flops=10**10, bytes_accessed=10**7, transcendentals=0),
    )(where, stacked, *pieces)


def moved(a, dy, dh, dc):
    perm = []
    for v in range(VOX):
        y, h, c = v // 4, (v // 2) % 2, v % 2
        perm.append((((y + dy) % 4) * 4 + (h ^ dh) * 2 + (c ^ dc), v))
    return lax.ppermute(a, "vox", perm)


PLACES = [(dy, dh, dc) for dy in range(4) for dh in range(2) for dc in range(2)]
WHOLE = [(0, 0), (1, 0), (3, 0), (0, 1)]
HALVES = [(1, 1), (3, 1), (2, 0), (2, 1)]


def part_list(rows):
    half = rows // 2
    listed = []
    for dc in range(2):
        listed += [(PLACES.index(k + (dc,)), 0, rows) for k in WHOLE]
        for k in HALVES:
            listed += [(PLACES.index(k + (dc,)), 0, half), (PLACES.index(k + (dc,)), half, half)]
    return listed


PIECE_LIST = part_list(STEP * SUBJ // 2)
DUAL_LIST = part_list(COLS)
PIECES = len(PIECE_LIST)


def gather_parts(own):
    half = own.shape[0] // 2
    up, down, side = moved(own, 1, 0, 0), moved(own, 3, 0, 0), moved(own, 0, 1, 0)
    twin = moved(own, 0, 0, 1)
    side_low = side[:half]
    side_up = [moved(side_low, 1, 0, 0), moved(up[half:], 0, 1, 0)]
    side_down = [moved(side_low, 3, 0, 0), moved(down[half:], 0, 1, 0)]
    far = [moved(up[:half], 1, 0, 0), moved(down[half:], 3, 0, 0)]
    side_far = [moved(side_up[0], 1, 0, 0), moved(side_down[1], 3, 0, 0)]
    parts = [up, down, side] + side_up + side_down + far + side_far
    return [own] + parts + [twin] + [moved(p, 0, 0, 1) for p in parts]


def lanczos(ticks, centers):
    distance = ticks[None, :] - centers[:, None]
    inside = jnp.abs(distance) < 3 * TICKS
    scaled = distance.astype(jnp.float32) / TICKS
    shaped = jnp.sinc(scaled) * jnp.sinc(scaled / 3.0)
    return jnp.where(inside, shaped, jnp.zeros_like(shaped)).astype(jnp.bfloat16)


def all_offsets(offsets, group):
    row = lax.broadcasted_iota(jnp.int32, (SUBJ, 128), 0)
    table = jnp.where(row == group, offsets[0], 0)
    for hop in (1, 2, 4):
        table = table + lax.ppermute(table, "subj", [(i, i ^ hop) for i in range(SUBJ)])
    return table[:, 0]


def body(features, token_ticks, offsets, run_lengths, penalty, responses):
    group = lax.axis_index("subj")
    vox = lax.axis_index("vox")
    core = vox % 2
    chip = group * CHIPS + vox // 2
    every = all_offsets(offsets, group)

    left, right = features[:, :HALF], features[:, HALF:]
    mine = jnp.where(core == 0, left, right)
    theirs = lax.ppermute(jnp.where(core == 0, right, left), "vox", [(i, i ^ 1) for i in range(VOX)])
    first = jnp.where(core == 0, mine, theirs)
    second = jnp.where(core == 0, theirs, mine)
    count = SUBJ * VOX
    before = lax.ppermute(second[-HALO:], ("subj", "vox"), [(i, i + 2) for i in range(count - 2)])
    after = lax.ppermute(first[:HALO], ("subj", "vox"), [(i + 2, i) for i in range(count - 2)])
    ext = jnp.concatenate([before, first, second, after], axis=0)
    far = jnp.full((HALO,), -(2**20), jnp.int32)
    span = ext.shape[0]
    near_ticks = lax.dynamic_slice_in_dim(
        jnp.concatenate([far, token_ticks, far]), chip * (span - 2 * HALO), span, 0
    )
    spread = (GAP / TICKS) ** 0.5
    steps = chip * STEP + jnp.arange(STEP, dtype=jnp.int32)
    centers = (steps[None, :] * TICKS + every[:, None]).reshape(-1)
    table = lanczos(near_ticks, centers)
    summed = jnp.dot(table, ext, preferred_element_type=jnp.float32)
    local = (summed * spread).astype(jnp.bfloat16).reshape(SUBJ, STEP, HALF)
    rows = lax.all_to_all(local, "subj", split_axis=0, concat_axis=0, tiled=True).reshape(SUBJ * STEP, HALF)
    cutrow = SUBJ * STEP // 2
    pieces = gather_parts(rows[:cutrow])
    gathered = lax.all_gather(rows[cutrow:], "vox", axis=0, tiled=False)

    lengths = run_lengths[0]
    starts = jnp.cumsum(lengths) - lengths
    tr_steps = jnp.arange(N, dtype=jnp.int32)
    run_first = jnp.max(jnp.where(starts[None, :] <= tr_steps[:, None], starts[None, :], 0), axis=1)
    pos = tr_steps - run_first
    row_pos, col_pos = pos[:, None], jnp.broadcast_to(pos[None, :], (8, N))
    y, h = vox // 4, (vox // 2) % 2
    where = jnp.stack([((y + dy) % 4) * 4 + (h ^ dh) * 2 + (core ^ dc) for dy, dh, dc in PLACES])
    *state, slab_first = first_call(where, penalty, pieces, responses[0].T, row_pos, col_pos)
    dual, slab_second = second_call(where, penalty, gathered, state, row_pos, col_pos)
    interp = jnp.concatenate([slab_first, slab_second], axis=0)
    delayed = []
    for k in range(1, DELAYS + 1):
        shifted = jnp.concatenate([jnp.zeros((k, SLAB), interp.dtype), interp[:-k]], axis=0)
        delayed.append(jnp.where((pos >= k)[:, None], shifted, jnp.zeros_like(shifted)))
    stacked = jnp.concatenate(delayed, axis=1).T
    projected = project_call(where, stacked, gather_parts(dual))
    return projected.reshape(1, DELAYS, SLAB, projected.shape[1])


def solution(mesh):
    return jax.shard_map(
        body,
        mesh=mesh,
        in_specs=(
            P(("subj", "vox"), None),
            P(),
            P("subj"),
            P("subj", None),
            P("subj"),
            P("subj", None, "vox"),
        ),
        out_specs=P("subj", None, "vox", None),
        check_vma=False,
    )
```

```python
import functools

import jax
import jax.numpy as jnp
from jax import lax
from jax.experimental import pallas as pl
from jax.experimental.pallas import tpu as pltpu
from jax.sharding import PartitionSpec as P

DELAYS = 4
TICKS = 64
GAP = 6
F = 4096
SUBJ = 8
VOX = 16
N = 1536
SLAB = F // VOX
COLS = 128
W = 256
PANELS = N // W
EDGE = 16
HALO = 32
VMEM_LIMIT = 52 * 2**20
STEP = 24
HALF = F // 2
CHIPS = 8
PART = N // 2
CUTP = PANELS // 2
HI = lax.Precision.HIGHEST
NT = (((1,), (1,)), ((), ()))


def mm(a, b):
    return jnp.dot(a, b, precision=HI, preferred_element_type=jnp.float32)


def mmt(a, b):
    return lax.dot_general(a, b, NT, precision=HI, preferred_element_type=jnp.float32)


def tree(terms):
    while len(terms) > 1:
        terms = [terms[i] + terms[i + 1] for i in range(0, len(terms), 2)]
    return terms[0]


def tri_inverse(block):
    rows = [block[8 * g : 8 * g + 8, :] for g in range(16)]
    shape = (8, 128)
    lane = lax.broadcasted_iota(jnp.int32, shape, 1)
    sub = lax.broadcasted_iota(jnp.int32, shape, 0)
    zero = jnp.where(lane + sub >= 1000, 1.0, 0.0)
    spot = [jnp.where(sub == p, 1.0, 0.0) for p in range(8)]

    def across(v, c):
        return jnp.broadcast_to(v[:, c : c + 1], shape)

    def down(v, r):
        return jnp.broadcast_to(v[r : r + 1, :], shape)

    def update(i, base, full):
        old = rows[i]
        inside = (lane >= base) & (lane < base + 8)
        rows[i] = jnp.where(inside, 0.0, old) - tree([across(old, base + q) * full[q] for q in range(8)])

    col = [across(rows[0], m) + zero for m in range(8)]
    pending = []
    for g in range(16):
        base = 8 * g
        inside = (lane >= base) & (lane < base + 8)
        u = jnp.where(inside, jnp.where(lane - base == sub, 1.0, 0.0), rows[g])
        out = u
        share = -(-len(pending) // 8)
        for p in range(8):
            pivot = down(col[p], p)
            root, inv = lax.rsqrt(pivot), 1.0 / pivot
            h = col[p] - spot[p]
            top = down(u, p)
            out = jnp.where(sub == p, top * root, out)
            u = u - (h * top) * inv
            for m in range(p + 1, 8):
                col[m] = col[m] - (h * down(col[m], p)) * inv
            for item in pending[p * share : (p + 1) * share]:
                update(*item)
        rows[g] = jnp.where(lane < base + 8, out, 0.0)
        if g == 15:
            break
        full = [down(u, m) for m in range(8)]
        update(g + 1, base, full)
        col = [across(rows[g + 1], base + 8 + m) + zero for m in range(8)]
        pending = [(i, base, full) for i in range(g + 2, 16)]
    return jnp.concatenate(rows, axis=0)


def cut(i, size=W):
    return pl.ds(pl.multiple_of(i * size, size), size)


def assemble(raw_ref, xs_ref, first):
    for g in range(SUBJ // 2):
        low = STEP * g // 16 * 16
        off = STEP * g - low

        def one(u, _, g=g, low=low, off=off):
            dest = pl.ds(pl.multiple_of(first + 192 * g + 48 * u, 16), 48)
            for c in range(2):
                pair = [
                    raw_ref[4 * u + 2 * e + c, low : low + 32, :].astype(jnp.float32)[off : off + STEP]
                    for e in range(2)
                ]
                xs_ref[dest, c * HALF : (c + 1) * HALF] = jnp.concatenate(pair, axis=0).astype(jnp.bfloat16)
            return 0

        lax.fori_loop(0, CHIPS // 2, one, 0)


def gram_rows(first, last, pen, xs_ref, a_ref, strip_ref, turn_ref, pr_ref, pc_ref):
    scale = 1.0 / (DELAYS * F)

    def gram(i, _):
        left = xs_ref[pl.ds(pl.multiple_of(i * W, W), W + EDGE), :]

        def one(j, _):
            right = xs_ref[pl.ds(pl.multiple_of(j * W + EDGE, EDGE), W), :]
            strip_ref[:, pl.ds(pl.multiple_of(j * W + 128, 128), W)] = lax.dot_general(
                left, right, NT, preferred_element_type=jnp.float32
            )
            return 0

        lax.fori_loop(0, i + 1, one, 0)
        row_pos = jnp.broadcast_to(pr_ref[cut(i), :], (W, 128))
        lane = lax.broadcasted_iota(jnp.int32, (W + EDGE, 128), 1)

        def shift(j, _):
            at = [pl.ds(pl.multiple_of(j * W + 128 * e, 128), 128) for e in range(3)]
            for e in range(2):
                back, here = strip_ref[:, at[e]], strip_ref[:, at[e + 1]]
                for k in range(1, DELAYS + 1):
                    turn_ref[k - 1, e] = pltpu.roll(jnp.where(lane >= 128 - k, back, here), k, 1)
            for e in range(2):
                near = jnp.minimum(row_pos, pc_ref[0:1, at[e]])
                parts = [
                    jnp.where(near >= k, turn_ref[k - 1, e, EDGE - k : EDGE - k + W, :], 0.0)
                    for k in range(1, DELAYS + 1)
                ]
                a_ref[cut(i), at[e]] = tree(parts) * scale
            return 0

        lax.fori_loop(0, i + 1, shift, 0)
        row = lax.broadcasted_iota(jnp.int32, (W, W), 0)
        column = lax.broadcasted_iota(jnp.int32, (W, W), 1)
        a_ref[cut(i), cut(i)] += jnp.where(row == column, pen, 0.0)
        return 0

    lax.fori_loop(first, last, gram, 0)


def diagonal(p, a_ref, inv_ref):
    def half(h, _):
        d = 2 * p + h
        blk = cut(d, 128)
        inv_ref[p, cut(h, 128), cut(h, 128)] = tri_inverse(a_ref[blk, blk])

        @pl.when(h == 0)
        def _():
            below = cut(d + 1, 128)
            c = mmt(a_ref[below, blk], inv_ref[p, 0:128, 0:128])
            a_ref[below, blk] = c
            a_ref[below, below] -= mmt(c, c)

        return 0

    lax.fori_loop(0, 2, half, 0)
    low = a_ref[cut(2 * p + 1, 128), cut(2 * p, 128)]
    inv_ref[p, 128:256, 0:128] = -mm(inv_ref[p, 128:256, 128:256], mm(low, inv_ref[p, 0:128, 0:128]))
    inv_ref[p, 0:128, 128:256] = jnp.zeros((128, 128), jnp.float32)


def eliminate(p, first, last, a_ref, inv_ref):
    here = cut(p)

    def scale_rows(i, _):
        a_ref[cut(i), here] = mmt(a_ref[cut(i), here], inv_ref[p])
        return 0

    lax.fori_loop(first, last, scale_rows, 0)

    def column(j, _):
        right = a_ref[cut(j), here]

        def update(i, _):
            a_ref[cut(i), cut(j)] -= mmt(a_ref[cut(i), here], right)
            return 0

        lax.fori_loop(jnp.maximum(j, first), last, update, 0)
        return 0

    lax.fori_loop(p + 1, last, column, 0)


def forward(p, first, last, a_ref, inv_ref, tail_ref):
    here = cut(p)

    def update(j, _):
        tail_ref[:, cut(j)] -= mmt(tail_ref[:, here], a_ref[cut(j), here])
        return 0

    lax.fori_loop(first, last, update, 0)


def first_kernel(*refs):
    (where_ref, pen_ref), refs = refs[:2], refs[2:]
    pieces, refs = refs[:PIECES], refs[PIECES:]
    b_ref, pr_ref, pc_ref, rows_out, low_out, inv_out, tail_out, slab_out = refs[:8]
    raw_ref, xs_ref, a_ref, strip_ref, turn_ref, inv_ref, tail_ref, sem = refs[8:]
    copies = []
    for n, (key, start, size) in enumerate(PIECE_LIST):
        copies.append(
            pltpu.make_async_copy(pieces[n], raw_ref.at[where_ref[key], pl.ds(start, size), :], sem.at[n])
        )
    copies.append(pltpu.make_async_copy(b_ref, tail_ref, sem.at[PIECES]))
    for c in copies:
        c.start()
    xs_ref[0:EDGE, :] = jnp.zeros((EDGE, F), jnp.bfloat16)
    strip_ref[:, 0:128] = jnp.zeros((W + EDGE, 128), jnp.float32)
    for c in copies:
        c.wait()
    assemble(raw_ref, xs_ref, EDGE)
    own = pl.ds(EDGE, PART)
    mine = pl.ds(pl.multiple_of(where_ref[0] * SLAB, SLAB), SLAB)
    outs = [
        pltpu.make_async_copy(xs_ref.at[own, :], rows_out, sem.at[PIECES + 1]),
        pltpu.make_async_copy(xs_ref.at[own, mine], slab_out, sem.at[PIECES + 2]),
    ]
    for c in outs:
        c.start()
    gram_rows(0, CUTP, pen_ref[0], xs_ref, a_ref, strip_ref, turn_ref, pr_ref, pc_ref)

    def panel(p, _):
        diagonal(p, a_ref, inv_ref)
        eliminate(p, p + 1, CUTP, a_ref, inv_ref)
        tail_ref[:, cut(p)] = mmt(tail_ref[:, cut(p)], inv_ref[p])
        forward(p, p + 1, CUTP, a_ref, inv_ref, tail_ref)
        return 0

    lax.fori_loop(0, CUTP, panel, 0)
    more = [
        pltpu.make_async_copy(a_ref, low_out, sem.at[PIECES + 3]),
        pltpu.make_async_copy(inv_ref, inv_out, sem.at[PIECES + 4]),
        pltpu.make_async_copy(tail_ref, tail_out, sem.at[PIECES + 5]),
    ]
    for c in more:
        c.start()
    for c in outs + more:
        c.wait()


def second_kernel(
    where_ref, pen_ref, all_ref, rows_in, low_in, inv_in, tail_in, pr_ref, pc_ref, o_ref, slab_out,
    raw_ref, xs_ref, a_ref, strip_ref, turn_ref, inv_ref, tail_ref, sem,
):
    chunk = pltpu.make_async_copy(all_ref, raw_ref, sem.at[0])
    copies = [
        pltpu.make_async_copy(rows_in, xs_ref.at[pl.ds(EDGE, PART), :], sem.at[1]),
        pltpu.make_async_copy(low_in, a_ref.at[pl.ds(0, PART), pl.ds(0, PART)], sem.at[2]),
        pltpu.make_async_copy(inv_in, inv_ref.at[pl.ds(0, CUTP)], sem.at[3]),
        pltpu.make_async_copy(tail_in, tail_ref, sem.at[4]),
    ]
    chunk.start()
    for c in copies:
        c.start()
    strip_ref[:, 0:128] = jnp.zeros((W + EDGE, 128), jnp.float32)
    chunk.wait()
    assemble(raw_ref, xs_ref, EDGE + PART)
    mine = pl.ds(pl.multiple_of(where_ref[0] * SLAB, SLAB), SLAB)
    slab = pltpu.make_async_copy(xs_ref.at[pl.ds(EDGE + PART, PART), mine], slab_out, sem.at[5])
    slab.start()
    for c in copies:
        c.wait()
    gram_rows(CUTP, PANELS, pen_ref[0], xs_ref, a_ref, strip_ref, turn_ref, pr_ref, pc_ref)

    for p in range(CUTP):
        here = slice(p * W, (p + 1) * W)
        new = mmt(a_ref[PART:N, here], inv_ref[p])
        a_ref[PART:N, here] = new
        for j in range(p + 1, PANELS):
            there = slice(j * W, (j + 1) * W)
            top = max(j * W - PART, 0)
            right = a_ref[there, here] if j < CUTP else new[top : top + W]
            a_ref[PART + top : N, there] -= mmt(new[top:], right)
        tail_ref[:, PART:N] -= mmt(tail_ref[:, here], new)

    def panel(p, _):
        diagonal(p, a_ref, inv_ref)
        eliminate(p, p + 1, PANELS, a_ref, inv_ref)
        tail_ref[:, cut(p)] = mmt(tail_ref[:, cut(p)], inv_ref[p])
        forward(p, p + 1, PANELS, a_ref, inv_ref, tail_ref)
        return 0

    lax.fori_loop(CUTP, PANELS, panel, 0)

    for p in reversed(range(PANELS)):
        here = slice(p * W, (p + 1) * W)
        x = mm(tail_ref[:, here], inv_ref[p])
        tail_ref[:, here] = x
        if p:
            tail_ref[:, : p * W] -= mm(x, a_ref[here, : p * W])
    o_ref[...] = tail_ref[...].astype(o_ref.dtype)
    slab.wait()


ANYWHERE = pl.BlockSpec(memory_space=pl.ANY)
IN_VMEM = pl.BlockSpec(memory_space=pltpu.VMEM)
IN_SMEM = pl.BlockSpec(memory_space=pltpu.SMEM)


def scratches(rows, sems):
    return [
        pltpu.VMEM((VOX, STEP * SUBJ // 2, HALF), jnp.bfloat16),
        pltpu.VMEM((rows + EDGE, F), jnp.bfloat16),
        pltpu.VMEM((rows, rows), jnp.float32),
        pltpu.VMEM((W + EDGE, rows + 128), jnp.float32),
        pltpu.VMEM((DELAYS, 2, W + EDGE, 128), jnp.float32),
        pltpu.VMEM((rows // W, W, W), jnp.float32),
        pltpu.VMEM((COLS, N), jnp.float32),
        pltpu.SemaphoreType.DMA((sems,)),
    ]


def first_call(where, pen, pieces, targets, row_pos, col_pos):
    return pl.pallas_call(
        first_kernel,
        out_shape=[
            jax.ShapeDtypeStruct((PART, F), jnp.bfloat16),
            jax.ShapeDtypeStruct((PART, PART), jnp.float32),
            jax.ShapeDtypeStruct((CUTP, W, W), jnp.float32),
            jax.ShapeDtypeStruct((COLS, N), jnp.float32),
            jax.ShapeDtypeStruct((PART, SLAB), jnp.bfloat16),
        ],
        in_specs=[IN_SMEM, IN_SMEM] + [ANYWHERE] * PIECES + [ANYWHERE, IN_VMEM, IN_VMEM],
        out_specs=[ANYWHERE] * 5,
        scratch_shapes=scratches(PART, PIECES + 6),
        compiler_params=pltpu.CompilerParams(vmem_limit_bytes=VMEM_LIMIT),
        cost_estimate=pl.CostEstimate(flops=3 * 10**10, bytes_accessed=2 * 10**7, transcendentals=0),
    )(where, pen, *pieces, targets, row_pos, col_pos)


def second_call(where, pen, gathered, state, row_pos, col_pos):
    return pl.pallas_call(
        second_kernel,
        out_shape=[
            jax.ShapeDtypeStruct((COLS, N), jnp.bfloat16),
            jax.ShapeDtypeStruct((PART, SLAB), jnp.bfloat16),
        ],
        in_specs=[IN_SMEM, IN_SMEM] + [ANYWHERE] * 5 + [IN_VMEM, IN_VMEM],
        out_specs=[IN_VMEM, ANYWHERE],
        scratch_shapes=scratches(N, 6),
        compiler_params=pltpu.CompilerParams(vmem_limit_bytes=VMEM_LIMIT),
        cost_estimate=pl.CostEstimate(flops=5 * 10**10, bytes_accessed=2 * 10**7, transcendentals=0),
    )(where, pen, gathered, *state, row_pos, col_pos)


def project_kernel(listed, *refs):
    where_ref, st_ref = refs[:2]
    count = len(listed)
    pieces, refs = refs[2 : 2 + count], refs[2 + count :]
    out_ref, xt_ref, buf_ref, sem, out_sem = refs[-5:]
    chips = []
    copies = {}
    for n, (key, start, size) in enumerate(listed):
        row = pl.multiple_of(where_ref[key] * COLS + start, 16)
        copy = pltpu.make_async_copy(pieces[n], xt_ref.at[pl.ds(row, size), :], sem.at[n])
        copy.start()
        copies.setdefault(key // 2, []).append(copy)
        if key // 2 not in chips:
            chips.append(key // 2)
    scale = (DELAYS * F) ** (-0.5)
    sent = []
    for n, chip in enumerate(chips):
        slot = n % 2
        for copy in copies[chip]:
            copy.wait()
        if n >= 2:
            sent[n - 2].wait()
        at = pl.ds(pl.multiple_of(where_ref[2 * chip] // 2 * W, W), W)
        got = lax.dot_general(st_ref[...], xt_ref[at, :], NT, preferred_element_type=jnp.float32)
        buf_ref[slot] = (got * scale).astype(jnp.bfloat16)
        sent.append(pltpu.make_async_copy(buf_ref.at[slot], out_ref.at[:, at], out_sem.at[slot]))
        sent[n].start()
    for c in sent[-2:]:
        c.wait()


def project_call(where, stacked, listed, pieces, begun=None):
    extra = [] if begun is None else [begun]
    return pl.pallas_call(
        functools.partial(project_kernel, listed),
        out_shape=jax.ShapeDtypeStruct((DELAYS * SLAB, VOX * COLS), jnp.bfloat16),
        in_specs=[IN_SMEM, IN_VMEM] + [ANYWHERE] * (len(pieces) + len(extra)),
        out_specs=ANYWHERE,
        scratch_shapes=[
            pltpu.VMEM((VOX * COLS, N), jnp.bfloat16),
            pltpu.VMEM((2, DELAYS * SLAB, W), jnp.bfloat16),
            pltpu.SemaphoreType.DMA((len(pieces),)),
            pltpu.SemaphoreType.DMA((2,)),
        ],
        input_output_aliases={2 + len(pieces): 0} if extra else {},
        compiler_params=pltpu.CompilerParams(vmem_limit_bytes=VMEM_LIMIT),
        cost_estimate=pl.CostEstimate(flops=5 * 10**9, bytes_accessed=7 * 10**6, transcendentals=0),
    )(where, stacked, *pieces, *extra)


def moved(a, dy, dh, dc):
    perm = []
    for v in range(VOX):
        y, h, c = v // 4, (v // 2) % 2, v % 2
        perm.append((((y + dy) % 4) * 4 + (h ^ dh) * 2 + (c ^ dc), v))
    return lax.ppermute(a, "vox", perm)


PLACES = [(dy, dh, dc) for dy in range(4) for dh in range(2) for dc in range(2)]
WHOLE = [(0, 0), (1, 0), (3, 0), (0, 1)]
HALVES = [(1, 1), (3, 1), (2, 0), (2, 1)]


def part_list(rows):
    half = rows // 2
    listed = []
    for dc in range(2):
        listed += [(PLACES.index(k + (dc,)), 0, rows) for k in WHOLE]
        for k in HALVES:
            listed += [(PLACES.index(k + (dc,)), 0, half), (PLACES.index(k + (dc,)), half, half)]
    return listed


PIECE_LIST = part_list(STEP * SUBJ // 2)
DUAL_LIST = part_list(COLS)
PIECES = len(PIECE_LIST)


def gather_parts(own):
    half = own.shape[0] // 2
    up, down, side = moved(own, 1, 0, 0), moved(own, 3, 0, 0), moved(own, 0, 1, 0)
    twin = moved(own, 0, 0, 1)
    side_low = side[:half]
    side_up = [moved(side_low, 1, 0, 0), moved(up[half:], 0, 1, 0)]
    side_down = [moved(side_low, 3, 0, 0), moved(down[half:], 0, 1, 0)]
    far = [moved(up[:half], 1, 0, 0), moved(down[half:], 3, 0, 0)]
    side_far = [moved(side_up[0], 1, 0, 0), moved(side_down[1], 3, 0, 0)]
    parts = [up, down, side] + side_up + side_down + far + side_far
    return [own] + parts + [twin] + [moved(p, 0, 0, 1) for p in parts]


def lanczos(ticks, centers):
    distance = ticks[None, :] - centers[:, None]
    inside = jnp.abs(distance) < 3 * TICKS
    scaled = distance.astype(jnp.float32) / TICKS
    shaped = jnp.sinc(scaled) * jnp.sinc(scaled / 3.0)
    return jnp.where(inside, shaped, jnp.zeros_like(shaped)).astype(jnp.bfloat16)


def all_offsets(offsets, group):
    row = lax.broadcasted_iota(jnp.int32, (SUBJ, 128), 0)
    table = jnp.where(row == group, offsets[0], 0)
    for hop in (1, 2, 4):
        table = table + lax.ppermute(table, "subj", [(i, i ^ hop) for i in range(SUBJ)])
    return table[:, 0]


def body(features, token_ticks, offsets, run_lengths, penalty, responses):
    group = lax.axis_index("subj")
    vox = lax.axis_index("vox")
    core = vox % 2
    chip = group * CHIPS + vox // 2
    left, right = features[:, :HALF], features[:, HALF:]
    mine = jnp.where(core == 0, left, right)
    theirs = lax.ppermute(jnp.where(core == 0, right, left), "vox", [(i, i ^ 1) for i in range(VOX)])
    offsets, theirs = lax.optimization_barrier((offsets, theirs))
    every = all_offsets(offsets, group)
    first = jnp.where(core == 0, mine, theirs)
    second = jnp.where(core == 0, theirs, mine)
    count = SUBJ * VOX
    before = lax.ppermute(second[-HALO:], ("subj", "vox"), [(i, i + 2) for i in range(count - 2)])
    after = lax.ppermute(first[:HALO], ("subj", "vox"), [(i + 2, i) for i in range(count - 2)])
    ext = jnp.concatenate([before, first, second, after], axis=0)
    far = jnp.full((HALO,), -(2**20), jnp.int32)
    span = ext.shape[0]
    near_ticks = lax.dynamic_slice_in_dim(
        jnp.concatenate([far, token_ticks, far]), chip * (span - 2 * HALO), span, 0
    )
    spread = (GAP / TICKS) ** 0.5
    steps = chip * STEP + jnp.arange(STEP, dtype=jnp.int32)
    centers = (steps[None, :] * TICKS + every[:, None]).reshape(-1)
    table = lanczos(near_ticks, centers)
    summed = jnp.dot(table, ext, preferred_element_type=jnp.float32)
    local = (summed * spread).astype(jnp.bfloat16).reshape(SUBJ, STEP, HALF)
    rows = lax.all_to_all(local, "subj", split_axis=0, concat_axis=0, tiled=True).reshape(SUBJ * STEP, HALF)
    cutrow = SUBJ * STEP // 2
    pieces = gather_parts(rows[:cutrow])
    later, pieces[3] = lax.optimization_barrier((rows[cutrow:], pieces[3]))
    gathered = lax.all_gather(later, "vox", axis=0, tiled=False)

    lengths = run_lengths[0]
    starts = jnp.cumsum(lengths) - lengths
    tr_steps = jnp.arange(N, dtype=jnp.int32)
    run_first = jnp.max(jnp.where(starts[None, :] <= tr_steps[:, None], starts[None, :], 0), axis=1)
    pos = tr_steps - run_first
    row_pos, col_pos = pos[:, None], jnp.broadcast_to(pos[None, :], (8, N))
    y, h = vox // 4, (vox // 2) % 2
    where = jnp.stack([((y + dy) % 4) * 4 + (h ^ dh) * 2 + (core ^ dc) for dy, dh, dc in PLACES])
    *state, slab_first = first_call(where, penalty, pieces, responses[0].T, row_pos, col_pos)
    dual, slab_second = second_call(where, penalty, gathered, state, row_pos, col_pos)
    interp = jnp.concatenate([slab_first, slab_second], axis=0)
    delayed = []
    for k in range(1, DELAYS + 1):
        shifted = jnp.concatenate([jnp.zeros((k, SLAB), interp.dtype), interp[:-k]], axis=0)
        delayed.append(jnp.where((pos >= k)[:, None], shifted, jnp.zeros_like(shifted)))
    stacked = jnp.concatenate(delayed, axis=1).T
    parts = gather_parts(dual)
    early = [n for n, item in enumerate(DUAL_LIST) if PLACES[item[0]][:2] in WHOLE]
    late = [n for n in range(PIECES) if n not in early]
    projected = None
    for chosen in (early, late):
        projected = project_call(
            where, stacked, [DUAL_LIST[n] for n in chosen], [parts[n] for n in chosen], projected
        )
    return projected.reshape(1, DELAYS, SLAB, projected.shape[1])


def solution(mesh):
    return jax.shard_map(
        body,
        mesh=mesh,
        in_specs=(
            P(("subj", "vox"), None),
            P(),
            P("subj"),
            P("subj", None),
            P("subj"),
            P("subj", None, "vox"),
        ),
        out_specs=P("subj", None, "vox", None),
        check_vma=False,
    )
```

```python
import functools

import jax
import jax.numpy as jnp
from jax import lax
from jax.experimental import pallas as pl
from jax.experimental.pallas import tpu as pltpu
from jax.sharding import PartitionSpec as P

DELAYS = 4
TICKS = 64
GAP = 6
F = 4096
SUBJ = 8
VOX = 16
N = 1536
SLAB = F // VOX
COLS = 128
W = 256
PANELS = N // W
EDGE = 16
HALO = 32
VMEM_LIMIT = 52 * 2**20
STEP = 24
HALF = F // 2
CHIPS = 8
PART = N // 2
CUTP = PANELS // 2
HI = lax.Precision.HIGHEST
NT = (((1,), (1,)), ((), ()))


def mm(a, b):
    return jnp.dot(a, b, precision=HI, preferred_element_type=jnp.float32)


def mmt(a, b):
    return lax.dot_general(a, b, NT, precision=HI, preferred_element_type=jnp.float32)


def tree(terms):
    while len(terms) > 1:
        terms = [terms[i] + terms[i + 1] for i in range(0, len(terms), 2)]
    return terms[0]


def tri_inverse(block):
    rows = [block[8 * g : 8 * g + 8, :] for g in range(16)]
    shape = (8, 128)
    lane = lax.broadcasted_iota(jnp.int32, shape, 1)
    sub = lax.broadcasted_iota(jnp.int32, shape, 0)
    zero = jnp.where(lane + sub >= 1000, 1.0, 0.0)
    spot = [jnp.where(sub == p, 1.0, 0.0) for p in range(8)]

    def across(v, c):
        return jnp.broadcast_to(v[:, c : c + 1], shape)

    def down(v, r):
        return jnp.broadcast_to(v[r : r + 1, :], shape)

    def update(i, base, full):
        old = rows[i]
        inside = (lane >= base) & (lane < base + 8)
        rows[i] = jnp.where(inside, 0.0, old) - tree([across(old, base + q) * full[q] for q in range(8)])

    col = [across(rows[0], m) + zero for m in range(8)]
    pending = []
    for g in range(16):
        base = 8 * g
        inside = (lane >= base) & (lane < base + 8)
        u = jnp.where(inside, jnp.where(lane - base == sub, 1.0, 0.0), rows[g])
        out = u
        share = -(-len(pending) // 8)
        for p in range(8):
            pivot = down(col[p], p)
            root, inv = lax.rsqrt(pivot), 1.0 / pivot
            h = col[p] - spot[p]
            top = down(u, p)
            out = jnp.where(sub == p, top * root, out)
            u = u - (h * top) * inv
            for m in range(p + 1, 8):
                col[m] = col[m] - (h * down(col[m], p)) * inv
            for item in pending[p * share : (p + 1) * share]:
                update(*item)
        rows[g] = jnp.where(lane < base + 8, out, 0.0)
        if g == 15:
            break
        full = [down(u, m) for m in range(8)]
        update(g + 1, base, full)
        col = [across(rows[g + 1], base + 8 + m) + zero for m in range(8)]
        pending = [(i, base, full) for i in range(g + 2, 16)]
    return jnp.concatenate(rows, axis=0)


def cut(i, size=W):
    return pl.ds(pl.multiple_of(i * size, size), size)


def assemble(raw_ref, xs_ref, first):
    for g in range(SUBJ // 2):
        low = STEP * g // 16 * 16
        off = STEP * g - low

        def one(u, _, g=g, low=low, off=off):
            dest = pl.ds(pl.multiple_of(first + 192 * g + 48 * u, 16), 48)
            for c in range(2):
                pair = [
                    raw_ref[4 * u + 2 * e + c, low : low + 32, :].astype(jnp.float32)[off : off + STEP]
                    for e in range(2)
                ]
                xs_ref[dest, c * HALF : (c + 1) * HALF] = jnp.concatenate(pair, axis=0).astype(jnp.bfloat16)
            return 0

        lax.fori_loop(0, CHIPS // 2, one, 0)


def gram_rows(first, last, pen, xs_ref, a_ref, strip_ref, turn_ref, pr_ref, pc_ref):
    scale = 1.0 / (DELAYS * F)

    def gram(i, _):
        left = xs_ref[pl.ds(pl.multiple_of(i * W, W), W + EDGE), :]

        def one(j, _):
            right = xs_ref[pl.ds(pl.multiple_of(j * W + EDGE, EDGE), W), :]
            strip_ref[:, pl.ds(pl.multiple_of(j * W + 128, 128), W)] = lax.dot_general(
                left, right, NT, preferred_element_type=jnp.float32
            )
            return 0

        lax.fori_loop(0, i + 1, one, 0)
        row_pos = jnp.broadcast_to(pr_ref[cut(i), :], (W, 128))
        lane = lax.broadcasted_iota(jnp.int32, (W + EDGE, 128), 1)

        def shift(j, _):
            at = [pl.ds(pl.multiple_of(j * W + 128 * e, 128), 128) for e in range(3)]
            for e in range(2):
                back, here = strip_ref[:, at[e]], strip_ref[:, at[e + 1]]
                for k in range(1, DELAYS + 1):
                    turn_ref[k - 1, e] = pltpu.roll(jnp.where(lane >= 128 - k, back, here), k, 1)
            for e in range(2):
                near = jnp.minimum(row_pos, pc_ref[0:1, at[e]])
                parts = [
                    jnp.where(near >= k, turn_ref[k - 1, e, EDGE - k : EDGE - k + W, :], 0.0)
                    for k in range(1, DELAYS + 1)
                ]
                a_ref[cut(i), at[e]] = tree(parts) * scale
            return 0

        lax.fori_loop(0, i + 1, shift, 0)
        row = lax.broadcasted_iota(jnp.int32, (W, W), 0)
        column = lax.broadcasted_iota(jnp.int32, (W, W), 1)
        a_ref[cut(i), cut(i)] += jnp.where(row == column, pen, 0.0)
        return 0

    lax.fori_loop(first, last, gram, 0)


def diagonal(p, a_ref, inv_ref):
    def half(h, _):
        d = 2 * p + h
        blk = cut(d, 128)
        inv_ref[p, cut(h, 128), cut(h, 128)] = tri_inverse(a_ref[blk, blk])

        @pl.when(h == 0)
        def _():
            below = cut(d + 1, 128)
            c = mmt(a_ref[below, blk], inv_ref[p, 0:128, 0:128])
            a_ref[below, blk] = c
            a_ref[below, below] -= mmt(c, c)

        return 0

    lax.fori_loop(0, 2, half, 0)
    low = a_ref[cut(2 * p + 1, 128), cut(2 * p, 128)]
    inv_ref[p, 128:256, 0:128] = -mm(inv_ref[p, 128:256, 128:256], mm(low, inv_ref[p, 0:128, 0:128]))
    inv_ref[p, 0:128, 128:256] = jnp.zeros((128, 128), jnp.float32)


def eliminate(p, first, last, a_ref, inv_ref):
    here = cut(p)

    def scale_rows(i, _):
        a_ref[cut(i), here] = mmt(a_ref[cut(i), here], inv_ref[p])
        return 0

    lax.fori_loop(first, last, scale_rows, 0)

    def column(j, _):
        right = a_ref[cut(j), here]

        def update(i, _):
            a_ref[cut(i), cut(j)] -= mmt(a_ref[cut(i), here], right)
            return 0

        lax.fori_loop(jnp.maximum(j, first), last, update, 0)
        return 0

    lax.fori_loop(p + 1, last, column, 0)


def forward(p, first, last, a_ref, inv_ref, tail_ref):
    here = cut(p)

    def update(j, _):
        tail_ref[:, cut(j)] -= mmt(tail_ref[:, here], a_ref[cut(j), here])
        return 0

    lax.fori_loop(first, last, update, 0)


def first_kernel(*refs):
    (where_ref, pen_ref), refs = refs[:2], refs[2:]
    pieces, refs = refs[:PIECES], refs[PIECES:]
    b_ref, pr_ref, pc_ref, rows_out, low_out, inv_out, tail_out, slab_out = refs[:8]
    raw_ref, xs_ref, a_ref, strip_ref, turn_ref, inv_ref, tail_ref, sem = refs[8:]
    copies = []
    for n, (ref, off, key, start, size) in enumerate(ROW_PARTS):
        source = pieces[ref].at[pl.ds(off, size), :]
        copies.append(pltpu.make_async_copy(source, raw_ref.at[where_ref[key], pl.ds(start, size), :], sem.at[n]))
    copies.append(pltpu.make_async_copy(b_ref, tail_ref, sem.at[PARTS]))
    for c in copies:
        c.start()
    xs_ref[0:EDGE, :] = jnp.zeros((EDGE, F), jnp.bfloat16)
    strip_ref[:, 0:128] = jnp.zeros((W + EDGE, 128), jnp.float32)
    for c in copies:
        c.wait()
    assemble(raw_ref, xs_ref, EDGE)
    own = pl.ds(EDGE, PART)
    mine = pl.ds(pl.multiple_of(where_ref[0] * SLAB, SLAB), SLAB)
    outs = [
        pltpu.make_async_copy(xs_ref.at[own, :], rows_out, sem.at[PARTS + 1]),
        pltpu.make_async_copy(xs_ref.at[own, mine], slab_out, sem.at[PARTS + 2]),
    ]
    for c in outs:
        c.start()
    gram_rows(0, CUTP, pen_ref[0], xs_ref, a_ref, strip_ref, turn_ref, pr_ref, pc_ref)

    def panel(p, _):
        diagonal(p, a_ref, inv_ref)
        eliminate(p, p + 1, CUTP, a_ref, inv_ref)
        tail_ref[:, cut(p)] = mmt(tail_ref[:, cut(p)], inv_ref[p])
        forward(p, p + 1, CUTP, a_ref, inv_ref, tail_ref)
        return 0

    lax.fori_loop(0, CUTP, panel, 0)
    more = [
        pltpu.make_async_copy(a_ref, low_out, sem.at[PARTS + 3]),
        pltpu.make_async_copy(inv_ref, inv_out, sem.at[PARTS + 4]),
        pltpu.make_async_copy(tail_ref, tail_out, sem.at[PARTS + 5]),
    ]
    for c in more:
        c.start()
    for c in outs + more:
        c.wait()


def second_kernel(
    where_ref, pen_ref, all_ref, rows_in, low_in, inv_in, tail_in, pr_ref, pc_ref, o_ref, slab_out,
    raw_ref, xs_ref, a_ref, strip_ref, turn_ref, inv_ref, tail_ref, sem,
):
    chunk = pltpu.make_async_copy(all_ref, raw_ref, sem.at[0])
    copies = [
        pltpu.make_async_copy(rows_in, xs_ref.at[pl.ds(EDGE, PART), :], sem.at[1]),
        pltpu.make_async_copy(low_in, a_ref.at[pl.ds(0, PART), pl.ds(0, PART)], sem.at[2]),
        pltpu.make_async_copy(inv_in, inv_ref.at[pl.ds(0, CUTP)], sem.at[3]),
        pltpu.make_async_copy(tail_in, tail_ref, sem.at[4]),
    ]
    chunk.start()
    for c in copies:
        c.start()
    strip_ref[:, 0:128] = jnp.zeros((W + EDGE, 128), jnp.float32)
    chunk.wait()
    assemble(raw_ref, xs_ref, EDGE + PART)
    mine = pl.ds(pl.multiple_of(where_ref[0] * SLAB, SLAB), SLAB)
    slab = pltpu.make_async_copy(xs_ref.at[pl.ds(EDGE + PART, PART), mine], slab_out, sem.at[5])
    slab.start()
    for c in copies:
        c.wait()
    gram_rows(CUTP, PANELS, pen_ref[0], xs_ref, a_ref, strip_ref, turn_ref, pr_ref, pc_ref)

    for p in range(CUTP):
        here = slice(p * W, (p + 1) * W)
        new = mmt(a_ref[PART:N, here], inv_ref[p])
        a_ref[PART:N, here] = new
        for j in range(p + 1, PANELS):
            there = slice(j * W, (j + 1) * W)
            top = max(j * W - PART, 0)
            right = a_ref[there, here] if j < CUTP else new[top : top + W]
            a_ref[PART + top : N, there] -= mmt(new[top:], right)
        tail_ref[:, PART:N] -= mmt(tail_ref[:, here], new)

    def panel(p, _):
        diagonal(p, a_ref, inv_ref)
        eliminate(p, p + 1, PANELS, a_ref, inv_ref)
        tail_ref[:, cut(p)] = mmt(tail_ref[:, cut(p)], inv_ref[p])
        forward(p, p + 1, PANELS, a_ref, inv_ref, tail_ref)
        return 0

    lax.fori_loop(CUTP, PANELS, panel, 0)

    for p in reversed(range(PANELS)):
        here = slice(p * W, (p + 1) * W)
        x = mm(tail_ref[:, here], inv_ref[p])
        tail_ref[:, here] = x
        if p:
            tail_ref[:, : p * W] -= mm(x, a_ref[here, : p * W])
    o_ref[...] = tail_ref[...].astype(o_ref.dtype)
    slab.wait()


ANYWHERE = pl.BlockSpec(memory_space=pl.ANY)
IN_VMEM = pl.BlockSpec(memory_space=pltpu.VMEM)
IN_SMEM = pl.BlockSpec(memory_space=pltpu.SMEM)


def scratches(rows, sems):
    return [
        pltpu.VMEM((VOX, STEP * SUBJ // 2, HALF), jnp.bfloat16),
        pltpu.VMEM((rows + EDGE, F), jnp.bfloat16),
        pltpu.VMEM((rows, rows), jnp.float32),
        pltpu.VMEM((W + EDGE, rows + 128), jnp.float32),
        pltpu.VMEM((DELAYS, 2, W + EDGE, 128), jnp.float32),
        pltpu.VMEM((rows // W, W, W), jnp.float32),
        pltpu.VMEM((COLS, N), jnp.float32),
        pltpu.SemaphoreType.DMA((sems,)),
    ]


def first_call(where, pen, pieces, targets, row_pos, col_pos):
    return pl.pallas_call(
        first_kernel,
        out_shape=[
            jax.ShapeDtypeStruct((PART, F), jnp.bfloat16),
            jax.ShapeDtypeStruct((PART, PART), jnp.float32),
            jax.ShapeDtypeStruct((CUTP, W, W), jnp.float32),
            jax.ShapeDtypeStruct((COLS, N), jnp.float32),
            jax.ShapeDtypeStruct((PART, SLAB), jnp.bfloat16),
        ],
        in_specs=[IN_SMEM, IN_SMEM] + [ANYWHERE] * PIECES + [ANYWHERE, IN_VMEM, IN_VMEM],
        out_specs=[ANYWHERE] * 5,
        scratch_shapes=scratches(PART, PARTS + 6),
        compiler_params=pltpu.CompilerParams(vmem_limit_bytes=VMEM_LIMIT),
        cost_estimate=pl.CostEstimate(flops=3 * 10**10, bytes_accessed=2 * 10**7, transcendentals=0),
    )(where, pen, *pieces, targets, row_pos, col_pos)


def second_call(where, pen, gathered, state, row_pos, col_pos):
    return pl.pallas_call(
        second_kernel,
        out_shape=[
            jax.ShapeDtypeStruct((COLS, N), jnp.bfloat16),
            jax.ShapeDtypeStruct((PART, SLAB), jnp.bfloat16),
        ],
        in_specs=[IN_SMEM, IN_SMEM] + [ANYWHERE] * 5 + [IN_VMEM, IN_VMEM],
        out_specs=[IN_VMEM, ANYWHERE],
        scratch_shapes=scratches(N, 6),
        compiler_params=pltpu.CompilerParams(vmem_limit_bytes=VMEM_LIMIT),
        cost_estimate=pl.CostEstimate(flops=5 * 10**10, bytes_accessed=2 * 10**7, transcendentals=0),
    )(where, pen, gathered, *state, row_pos, col_pos)


def project_kernel(where_ref, st_ref, *refs):
    pieces, (out_ref, xt_ref, buf_ref, sem, out_sem) = refs[:PIECES], refs[PIECES:]
    copies = []
    for n, (ref, off, key, start, size) in enumerate(DUAL_PARTS):
        row = pl.multiple_of(where_ref[key] * COLS + start, 16)
        source = pieces[ref].at[pl.ds(off, size), :]
        copies.append(pltpu.make_async_copy(source, xt_ref.at[pl.ds(row, size), :], sem.at[n]))
    for c in copies:
        c.start()
    for c in copies:
        c.wait()
    scale = (DELAYS * F) ** (-0.5)
    sent = []
    for n in range(DELAYS * SLAB // W):
        slot = n % 2
        at = slice(n * W, (n + 1) * W)
        if n >= 2:
            sent[n - 2].wait()
        got = lax.dot_general(st_ref[at, :], xt_ref[...], NT, preferred_element_type=jnp.float32)
        buf_ref[slot] = (got * scale).astype(jnp.bfloat16)
        sent.append(pltpu.make_async_copy(buf_ref.at[slot], out_ref.at[at, :], out_sem.at[slot]))
        sent[n].start()
    for c in sent[-2:]:
        c.wait()


def project_call(where, stacked, pieces):
    return pl.pallas_call(
        project_kernel,
        out_shape=jax.ShapeDtypeStruct((DELAYS * SLAB, VOX * COLS), jnp.bfloat16),
        in_specs=[IN_SMEM, IN_VMEM] + [ANYWHERE] * PIECES,
        out_specs=ANYWHERE,
        scratch_shapes=[
            pltpu.VMEM((VOX * COLS, N), jnp.bfloat16),
            pltpu.VMEM((2, W, VOX * COLS), jnp.bfloat16),
            pltpu.SemaphoreType.DMA((PARTS,)),
            pltpu.SemaphoreType.DMA((2,)),
        ],
        compiler_params=pltpu.CompilerParams(vmem_limit_bytes=VMEM_LIMIT),
        cost_estimate=pl.CostEstimate(flops=10**10, bytes_accessed=10**7, transcendentals=0),
    )(where, stacked, *pieces)


def moved(a, dy, dh, dc):
    perm = []
    for v in range(VOX):
        y, h, c = v // 4, (v // 2) % 2, v % 2
        perm.append((((y + dy) % 4) * 4 + (h ^ dh) * 2 + (c ^ dc), v))
    return lax.ppermute(a, "vox", perm)


PLACES = [(dy, dh, dc) for dy in range(4) for dh in range(2) for dc in range(2)]
PIECES = 13


def part_list(n):
    h = n // 2
    whole = [(1, 0), (3, 0), (0, 1)]
    split = [[(1, 1), 0, (2, 0), 0], [(3, 1), 0, (2, 0), h], [(1, 1), h, (3, 1), h]]
    listed = []
    for dc in range(2):
        at = [PLACES.index(k + (dc,)) for k in whole]
        listed.append((9 * dc, 0, PLACES.index((0, 0, dc)), 0, n))
        for e in range(3):
            listed.append((1 + e, 0, at[e], 0, n) if dc == 0 else (10, e * n, at[e], 0, n))
        for e, (first, low, second, high) in enumerate(split):
            ref, off = (4 + e, 0) if dc == 0 else (11, e * n)
            listed.append((ref, off, PLACES.index(first + (dc,)), low, h))
            listed.append((ref, off + h, PLACES.index(second + (dc,)), high, h))
        last = PLACES.index((2, 1, dc))
        listed.append((7, 0, last, 0, h) if dc == 0 else (12, 0, last, 0, h))
        listed.append((8, 0, last, h, h) if dc == 0 else (12, h, last, h, h))
    return listed


ROW_PARTS = part_list(STEP * SUBJ // 2)
DUAL_PARTS = part_list(COLS)
PARTS = len(ROW_PARTS)


def gather_parts(own):
    half = own.shape[0] // 2
    up, down, side = moved(own, 1, 0, 0), moved(own, 3, 0, 0), moved(own, 0, 1, 0)
    twin = moved(own, 0, 0, 1)
    join = functools.partial(jnp.concatenate, axis=0)
    from_up = moved(join([side[:half], up[:half]]), 1, 0, 0)
    from_down = moved(join([side[:half], down[half:]]), 3, 0, 0)
    from_side = moved(join([up[half:], down[half:]]), 0, 1, 0)
    far_up, far_down = moved(from_up[:half], 1, 0, 0), moved(from_side[half:], 3, 0, 0)
    twin_first = moved(join([up, down, side]), 0, 0, 1)
    twin_second = moved(join([from_up, from_down, from_side]), 0, 0, 1)
    twin_third = moved(join([far_up, far_down]), 0, 0, 1)
    return [own, up, down, side, from_up, from_down, from_side, far_up, far_down] + [
        twin, twin_first, twin_second, twin_third,
    ]


def lanczos(ticks, centers):
    distance = ticks[None, :] - centers[:, None]
    inside = jnp.abs(distance) < 3 * TICKS
    scaled = distance.astype(jnp.float32) / TICKS
    shaped = jnp.sinc(scaled) * jnp.sinc(scaled / 3.0)
    return jnp.where(inside, shaped, jnp.zeros_like(shaped)).astype(jnp.bfloat16)


def all_offsets(offsets, group):
    row = lax.broadcasted_iota(jnp.int32, (SUBJ, 128), 0)
    table = jnp.where(row == group, offsets[0], 0)
    table = table + lax.ppermute(table, "subj", [(i, i ^ 1) for i in range(SUBJ)])
    rest = [lax.ppermute(table, "subj", [(i, i ^ hop) for i in range(SUBJ)]) for hop in (2, 4, 6)]
    return (table + rest[0] + rest[1] + rest[2])[:, 0]


def body(features, token_ticks, offsets, run_lengths, penalty, responses):
    group = lax.axis_index("subj")
    vox = lax.axis_index("vox")
    core = vox % 2
    chip = group * CHIPS + vox // 2
    left, right = features[:, :HALF], features[:, HALF:]
    mine = jnp.where(core == 0, left, right)
    theirs = lax.ppermute(jnp.where(core == 0, right, left), "vox", [(i, i ^ 1) for i in range(VOX)])
    every = all_offsets(offsets + (theirs[0, 0] * 0).astype(jnp.int32), group)
    first = jnp.where(core == 0, mine, theirs)
    second = jnp.where(core == 0, theirs, mine)
    count = SUBJ * VOX
    before = lax.ppermute(second[-HALO:], ("subj", "vox"), [(i, i + 2) for i in range(count - 2)])
    after = lax.ppermute(first[:HALO], ("subj", "vox"), [(i + 2, i) for i in range(count - 2)])
    ext = jnp.concatenate([before, first, second, after], axis=0)
    far = jnp.full((HALO,), -(2**20), jnp.int32)
    span = ext.shape[0]
    near_ticks = lax.dynamic_slice_in_dim(
        jnp.concatenate([far, token_ticks, far]), chip * (span - 2 * HALO), span, 0
    )
    spread = (GAP / TICKS) ** 0.5
    steps = chip * STEP + jnp.arange(STEP, dtype=jnp.int32)
    centers = (steps[None, :] * TICKS + every[:, None]).reshape(-1)
    table = lanczos(near_ticks, centers)
    summed = jnp.dot(table, ext, preferred_element_type=jnp.float32)
    local = (summed * spread).astype(jnp.bfloat16).reshape(SUBJ, STEP, HALF)
    rows = lax.all_to_all(local, "subj", split_axis=0, concat_axis=0, tiled=True).reshape(SUBJ * STEP, HALF)
    cutrow = SUBJ * STEP // 2
    pieces = gather_parts(rows[:cutrow])
    gathered = lax.all_gather(rows[cutrow:] + sum(p[:1, :1] for p in pieces[1:4]) * 0, "vox", axis=0, tiled=False)

    lengths = run_lengths[0]
    starts = jnp.cumsum(lengths) - lengths
    tr_steps = jnp.arange(N, dtype=jnp.int32)
    run_first = jnp.max(jnp.where(starts[None, :] <= tr_steps[:, None], starts[None, :], 0), axis=1)
    pos = tr_steps - run_first
    row_pos, col_pos = pos[:, None], jnp.broadcast_to(pos[None, :], (8, N))
    y, h = vox // 4, (vox // 2) % 2
    where = jnp.stack([((y + dy) % 4) * 4 + (h ^ dh) * 2 + (core ^ dc) for dy, dh, dc in PLACES])
    *state, slab_first = first_call(where, penalty, pieces, responses[0].T, row_pos, col_pos)
    dual, slab_second = second_call(where, penalty, gathered, state, row_pos, col_pos)
    interp = jnp.concatenate([slab_first, slab_second], axis=0)
    delayed = []
    for k in range(1, DELAYS + 1):
        shifted = jnp.concatenate([jnp.zeros((k, SLAB), interp.dtype), interp[:-k]], axis=0)
        delayed.append(jnp.where((pos >= k)[:, None], shifted, jnp.zeros_like(shifted)))
    stacked = jnp.concatenate(delayed, axis=1).T
    projected = project_call(where, stacked, gather_parts(dual))
    return projected.reshape(1, DELAYS, SLAB, projected.shape[1])


def solution(mesh):
    return jax.shard_map(
        body,
        mesh=mesh,
        in_specs=(
            P(("subj", "vox"), None),
            P(),
            P("subj"),
            P("subj", None),
            P("subj"),
            P("subj", None, "vox"),
        ),
        out_specs=P("subj", None, "vox", None),
        check_vma=False,
    )
```

```python
import functools

import jax
import jax.numpy as jnp
from jax import lax
from jax.experimental import pallas as pl
from jax.experimental.pallas import tpu as pltpu
from jax.sharding import PartitionSpec as P

DELAYS = 4
TICKS = 64
GAP = 6
F = 4096
SUBJ = 8
VOX = 16
N = 1536
SLAB = F // VOX
COLS = 128
W = 256
PANELS = N // W
EDGE = 16
HALO = 32
VMEM_LIMIT = 52 * 2**20
STEP = 24
HALF = F // 2
CHIPS = 8
PART = N // 2
CUTP = PANELS // 2
HI = lax.Precision.HIGHEST
NT = (((1,), (1,)), ((), ()))


def mm(a, b):
    return jnp.dot(a, b, precision=HI, preferred_element_type=jnp.float32)


def mmt(a, b):
    return lax.dot_general(a, b, NT, precision=HI, preferred_element_type=jnp.float32)


def tree(terms):
    while len(terms) > 1:
        terms = [terms[i] + terms[i + 1] for i in range(0, len(terms), 2)]
    return terms[0]


def tri_inverse(block):
    rows = [block[8 * g : 8 * g + 8, :] for g in range(16)]
    shape = (8, 128)
    lane = lax.broadcasted_iota(jnp.int32, shape, 1)
    sub = lax.broadcasted_iota(jnp.int32, shape, 0)
    zero = jnp.where(lane + sub >= 1000, 1.0, 0.0)
    spot = [jnp.where(sub == p, 1.0, 0.0) for p in range(8)]
    none = jnp.zeros(shape, jnp.float32)

    def across(v, c):
        return jnp.broadcast_to(v[:, c : c + 1], shape)

    def down(v, r):
        return jnp.broadcast_to(v[r : r + 1, :], shape)

    def inside(low, high):
        return (lane >= low) & (lane < high)

    def pivots(row, base, col, extra):
        u = jnp.where(inside(base, base + 8), jnp.where(lane - base == sub, 1.0, 0.0), row)
        out = u
        for p in range(8):
            pivot = down(col[p], p)
            root, inv = lax.rsqrt(pivot), 1.0 / pivot
            h = col[p] - spot[p]
            top = down(u, p)
            out = jnp.where(sub == p, top * root, out)
            u = u - (h * top) * inv
            for m in range(p + 1, 8):
                col[m] = col[m] - (h * down(col[m], p)) * inv
            for m in range(len(extra)):
                extra[m] = extra[m] - (h * down(extra[m], p)) * inv
        return u, out

    def minus(row, low, high, factors, full):
        return jnp.where(inside(low, high), 0.0, row) - tree([f * v for f, v in zip(factors, full)])

    far = None
    for g in range(0, 16, 2):
        base = 8 * g
        first, second = rows[g], rows[g + 1]
        col = [across(first, base + m) + zero for m in range(8)]
        side = [across(second, base + q) for q in range(8)]
        if far is not None:
            ids, low, left, right = far
            later = mm(left, right)
        ahead = [across(first, base + 8 + m) + zero for m in range(8)]
        diag = [across(second, base + 8 + m) for m in range(8)]
        u, out = pivots(first, base, col, ahead)
        rows[g] = jnp.where(lane < base + 8, out, 0.0)
        col = [diag[m] - tree([side[q] * down(ahead[m], q) for q in range(8)]) for m in range(8)]
        second = minus(second, base, base + 8, side, [down(u, q) for q in range(8)])
        cross = [across(u, base + 8 + q) for q in range(8)]
        v, out = pivots(second, base + 8, col, [])
        rows[g + 1] = jnp.where(lane < base + 16, out, 0.0)
        if far is not None:
            for n, i in enumerate(ids):
                rows[i] = jnp.where(inside(low, low + 16), 0.0, rows[i]) - later[8 * n : 8 * n + 8]
            far = None
        if g == 14:
            break
        u = minus(u, base + 8, base + 16, cross, [down(v, q) for q in range(8)])
        full = [down(u, q) for q in range(8)] + [down(v, q) for q in range(8)]
        ids = list(range(g + 4, 16))
        if ids:
            left = jnp.concatenate([rows[i] for i in ids], axis=0)
            right = jnp.concatenate([none] * g + [u, v] + [none] * (14 - g), axis=0)
            far = (ids, base, left, right)
        for i in (g + 2, g + 3):
            factors = [across(rows[i], base + q) for q in range(16)]
            rows[i] = minus(rows[i], base, base + 16, factors, full)
    return jnp.concatenate(rows, axis=0)


def cut(i, size=W):
    return pl.ds(pl.multiple_of(i * size, size), size)


def assemble(raw_ref, xs_ref, first):
    for g in range(SUBJ // 2):
        low = STEP * g // 16 * 16
        off = STEP * g - low

        def one(u, _, g=g, low=low, off=off):
            dest = pl.ds(pl.multiple_of(first + 192 * g + 48 * u, 16), 48)
            for c in range(2):
                pair = [
                    raw_ref[4 * u + 2 * e + c, low : low + 32, :].astype(jnp.float32)[off : off + STEP]
                    for e in range(2)
                ]
                xs_ref[dest, c * HALF : (c + 1) * HALF] = jnp.concatenate(pair, axis=0).astype(jnp.bfloat16)
            return 0

        lax.fori_loop(0, CHIPS // 2, one, 0)


def gram_rows(first, last, pen, xs_ref, a_ref, strip_ref, turn_ref, pr_ref, pc_ref):
    scale = 1.0 / (DELAYS * F)

    def gram(i, _):
        left = xs_ref[pl.ds(pl.multiple_of(i * W, W), W + EDGE), :]

        def one(j):
            right = xs_ref[pl.ds(pl.multiple_of(j * W + EDGE, EDGE), W), :]
            strip_ref[:, pl.ds(pl.multiple_of(j * W + 128, 128), W)] = lax.dot_general(
                left, right, NT, preferred_element_type=jnp.float32
            )

        row_pos = jnp.broadcast_to(pr_ref[cut(i), :], (W, 128))
        lane = lax.broadcasted_iota(jnp.int32, (W + EDGE, 128), 1)

        def shift(j):
            at = [pl.ds(pl.multiple_of(j * W + 128 * e, 128), 128) for e in range(3)]
            for e in range(2):
                back, here = strip_ref[:, at[e]], strip_ref[:, at[e + 1]]
                for k in range(1, DELAYS + 1):
                    turn_ref[k - 1, e] = pltpu.roll(jnp.where(lane >= 128 - k, back, here), k, 1)
            for e in range(2):
                near = jnp.minimum(row_pos, pc_ref[0:1, at[e]])
                parts = [
                    jnp.where(near >= k, turn_ref[k - 1, e, EDGE - k : EDGE - k + W, :], 0.0)
                    for k in range(1, DELAYS + 1)
                ]
                a_ref[cut(i), at[e]] = tree(parts) * scale

        def both(j, _):
            shift(j - 1)
            one(j)
            return 0

        one(0)
        lax.fori_loop(1, i + 1, both, 0)
        shift(i)
        row = lax.broadcasted_iota(jnp.int32, (W, W), 0)
        column = lax.broadcasted_iota(jnp.int32, (W, W), 1)
        a_ref[cut(i), cut(i)] += jnp.where(row == column, pen, 0.0)
        return 0

    lax.fori_loop(first, last, gram, 0)


def diagonal(p, a_ref, inv_ref):
    top, below = cut(2 * p, 128), cut(2 * p + 1, 128)
    first = tri_inverse(a_ref[top, top])
    c = mmt(a_ref[below, top], first)
    turned = mm(c, first)
    second = tri_inverse(a_ref[below, below] - mmt(c, c))
    inv_ref[p, 0:128, 0:128] = first
    inv_ref[p, 128:256, 128:256] = second
    inv_ref[p, 128:256, 0:128] = -mm(second, turned)
    inv_ref[p, 0:128, 128:256] = jnp.zeros((128, 128), jnp.float32)


def eliminate(p, first, last, a_ref, inv_ref):
    here = cut(p)

    def scale_rows(i, _):
        a_ref[cut(i), here] = mmt(a_ref[cut(i), here], inv_ref[p])
        return 0

    lax.fori_loop(first, last, scale_rows, 0)

    def column(j, _):
        right = a_ref[cut(j), here]

        def update(i, _):
            a_ref[cut(i), cut(j)] -= mmt(a_ref[cut(i), here], right)
            return 0

        lax.fori_loop(jnp.maximum(j, first), last, update, 0)
        return 0

    lax.fori_loop(p + 1, last, column, 0)


def forward(p, first, last, a_ref, inv_ref, tail_ref):
    here = cut(p)

    def update(j, _):
        tail_ref[:, cut(j)] -= mmt(tail_ref[:, here], a_ref[cut(j), here])
        return 0

    lax.fori_loop(first, last, update, 0)


def first_kernel(*refs):
    (where_ref, pen_ref), refs = refs[:2], refs[2:]
    pieces, refs = refs[:PIECES], refs[PIECES:]
    b_ref, pr_ref, pc_ref, rows_out, low_out, inv_out, tail_out, slab_out = refs[:8]
    raw_ref, xs_ref, a_ref, strip_ref, turn_ref, inv_ref, tail_ref, sem = refs[8:]
    copies = []
    for n, (ref, off, key, start, size) in enumerate(ROW_PARTS):
        source = pieces[ref].at[pl.ds(off, size), :]
        copies.append(pltpu.make_async_copy(source, raw_ref.at[where_ref[key], pl.ds(start, size), :], sem.at[n]))
    copies.append(pltpu.make_async_copy(b_ref, tail_ref, sem.at[PARTS]))
    for c in copies:
        c.start()
    xs_ref[0:EDGE, :] = jnp.zeros((EDGE, F), jnp.bfloat16)
    strip_ref[:, 0:128] = jnp.zeros((W + EDGE, 128), jnp.float32)
    for c in copies:
        c.wait()
    assemble(raw_ref, xs_ref, EDGE)
    own = pl.ds(EDGE, PART)
    mine = pl.ds(pl.multiple_of(where_ref[0] * SLAB, SLAB), SLAB)
    outs = [
        pltpu.make_async_copy(xs_ref.at[own, :], rows_out, sem.at[PARTS + 1]),
        pltpu.make_async_copy(xs_ref.at[own, mine], slab_out, sem.at[PARTS + 2]),
    ]
    for c in outs:
        c.start()
    gram_rows(0, CUTP, pen_ref[0], xs_ref, a_ref, strip_ref, turn_ref, pr_ref, pc_ref)

    def panel(p, _):
        diagonal(p, a_ref, inv_ref)
        eliminate(p, p + 1, CUTP, a_ref, inv_ref)
        tail_ref[:, cut(p)] = mmt(tail_ref[:, cut(p)], inv_ref[p])
        forward(p, p + 1, CUTP, a_ref, inv_ref, tail_ref)
        return 0

    lax.fori_loop(0, CUTP, panel, 0)
    more = [
        pltpu.make_async_copy(a_ref, low_out, sem.at[PARTS + 3]),
        pltpu.make_async_copy(inv_ref, inv_out, sem.at[PARTS + 4]),
        pltpu.make_async_copy(tail_ref, tail_out, sem.at[PARTS + 5]),
    ]
    for c in more:
        c.start()
    for c in outs + more:
        c.wait()


def second_kernel(
    where_ref, pen_ref, all_ref, rows_in, low_in, inv_in, tail_in, pr_ref, pc_ref, o_ref, slab_out,
    raw_ref, xs_ref, a_ref, strip_ref, turn_ref, inv_ref, tail_ref, sem,
):
    chunk = pltpu.make_async_copy(all_ref, raw_ref, sem.at[0])
    copies = [
        pltpu.make_async_copy(rows_in, xs_ref.at[pl.ds(EDGE, PART), :], sem.at[1]),
        pltpu.make_async_copy(low_in, a_ref.at[pl.ds(0, PART), pl.ds(0, PART)], sem.at[2]),
        pltpu.make_async_copy(inv_in, inv_ref.at[pl.ds(0, CUTP)], sem.at[3]),
        pltpu.make_async_copy(tail_in, tail_ref, sem.at[4]),
    ]
    chunk.start()
    for c in copies:
        c.start()
    strip_ref[:, 0:128] = jnp.zeros((W + EDGE, 128), jnp.float32)
    chunk.wait()
    assemble(raw_ref, xs_ref, EDGE + PART)
    mine = pl.ds(pl.multiple_of(where_ref[0] * SLAB, SLAB), SLAB)
    slab = pltpu.make_async_copy(xs_ref.at[pl.ds(EDGE + PART, PART), mine], slab_out, sem.at[5])
    slab.start()
    for c in copies:
        c.wait()
    gram_rows(CUTP, PANELS, pen_ref[0], xs_ref, a_ref, strip_ref, turn_ref, pr_ref, pc_ref)

    for p in range(CUTP):
        here = slice(p * W, (p + 1) * W)
        new = mmt(a_ref[PART:N, here], inv_ref[p])
        a_ref[PART:N, here] = new
        for j in range(p + 1, PANELS):
            there = slice(j * W, (j + 1) * W)
            top = max(j * W - PART, 0)
            right = a_ref[there, here] if j < CUTP else new[top : top + W]
            a_ref[PART + top : N, there] -= mmt(new[top:], right)
        tail_ref[:, PART:N] -= mmt(tail_ref[:, here], new)

    def panel(p, _):
        diagonal(p, a_ref, inv_ref)
        eliminate(p, p + 1, PANELS, a_ref, inv_ref)
        tail_ref[:, cut(p)] = mmt(tail_ref[:, cut(p)], inv_ref[p])
        forward(p, p + 1, PANELS, a_ref, inv_ref, tail_ref)
        return 0

    lax.fori_loop(CUTP, PANELS, panel, 0)

    for p in reversed(range(PANELS)):
        here = slice(p * W, (p + 1) * W)
        x = mm(tail_ref[:, here], inv_ref[p])
        tail_ref[:, here] = x
        if p:
            tail_ref[:, : p * W] -= mm(x, a_ref[here, : p * W])
    o_ref[...] = tail_ref[...].astype(o_ref.dtype)
    slab.wait()


ANYWHERE = pl.BlockSpec(memory_space=pl.ANY)
IN_VMEM = pl.BlockSpec(memory_space=pltpu.VMEM)
IN_SMEM = pl.BlockSpec(memory_space=pltpu.SMEM)


def scratches(rows, sems):
    return [
        pltpu.VMEM((VOX, STEP * SUBJ // 2, HALF), jnp.bfloat16),
        pltpu.VMEM((rows + EDGE, F), jnp.bfloat16),
        pltpu.VMEM((rows, rows), jnp.float32),
        pltpu.VMEM((W + EDGE, rows + 128), jnp.float32),
        pltpu.VMEM((DELAYS, 2, W + EDGE, 128), jnp.float32),
        pltpu.VMEM((rows // W, W, W), jnp.float32),
        pltpu.VMEM((COLS, N), jnp.float32),
        pltpu.SemaphoreType.DMA((sems,)),
    ]


def first_call(where, pen, pieces, targets, row_pos, col_pos):
    return pl.pallas_call(
        first_kernel,
        out_shape=[
            jax.ShapeDtypeStruct((PART, F), jnp.bfloat16),
            jax.ShapeDtypeStruct((PART, PART), jnp.float32),
            jax.ShapeDtypeStruct((CUTP, W, W), jnp.float32),
            jax.ShapeDtypeStruct((COLS, N), jnp.float32),
            jax.ShapeDtypeStruct((PART, SLAB), jnp.bfloat16),
        ],
        in_specs=[IN_SMEM, IN_SMEM] + [ANYWHERE] * PIECES + [ANYWHERE, IN_VMEM, IN_VMEM],
        out_specs=[ANYWHERE] * 5,
        scratch_shapes=scratches(PART, PARTS + 6),
        compiler_params=pltpu.CompilerParams(vmem_limit_bytes=VMEM_LIMIT),
        cost_estimate=pl.CostEstimate(flops=3 * 10**10, bytes_accessed=2 * 10**7, transcendentals=0),
    )(where, pen, *pieces, targets, row_pos, col_pos)


def second_call(where, pen, gathered, state, row_pos, col_pos):
    return pl.pallas_call(
        second_kernel,
        out_shape=[
            jax.ShapeDtypeStruct((COLS, N), jnp.bfloat16),
            jax.ShapeDtypeStruct((PART, SLAB), jnp.bfloat16),
        ],
        in_specs=[IN_SMEM, IN_SMEM] + [ANYWHERE] * 5 + [IN_VMEM, IN_VMEM],
        out_specs=[IN_VMEM, ANYWHERE],
        scratch_shapes=scratches(N, 6),
        compiler_params=pltpu.CompilerParams(vmem_limit_bytes=VMEM_LIMIT),
        cost_estimate=pl.CostEstimate(flops=5 * 10**10, bytes_accessed=2 * 10**7, transcendentals=0),
    )(where, pen, gathered, *state, row_pos, col_pos)


def project_kernel(where_ref, st_ref, *refs):
    pieces, (out_ref, xt_ref, buf_ref, sem, out_sem) = refs[:PIECES], refs[PIECES:]
    copies = []
    for n, (ref, off, key, start, size) in enumerate(DUAL_PARTS):
        row = pl.multiple_of(where_ref[key] * COLS + start, 16)
        source = pieces[ref].at[pl.ds(off, size), :]
        copies.append(pltpu.make_async_copy(source, xt_ref.at[pl.ds(row, size), :], sem.at[n]))
    for c in copies:
        c.start()
    for c in copies:
        c.wait()
    scale = (DELAYS * F) ** (-0.5)
    sent = []
    for n in range(DELAYS * SLAB // W):
        slot = n % 2
        at = slice(n * W, (n + 1) * W)
        if n >= 2:
            sent[n - 2].wait()
        got = lax.dot_general(st_ref[at, :], xt_ref[...], NT, preferred_element_type=jnp.float32)
        buf_ref[slot] = (got * scale).astype(jnp.bfloat16)
        sent.append(pltpu.make_async_copy(buf_ref.at[slot], out_ref.at[at, :], out_sem.at[slot]))
        sent[n].start()
    for c in sent[-2:]:
        c.wait()


def project_call(where, stacked, pieces):
    return pl.pallas_call(
        project_kernel,
        out_shape=jax.ShapeDtypeStruct((DELAYS * SLAB, VOX * COLS), jnp.bfloat16),
        in_specs=[IN_SMEM, IN_VMEM] + [ANYWHERE] * PIECES,
        out_specs=ANYWHERE,
        scratch_shapes=[
            pltpu.VMEM((VOX * COLS, N), jnp.bfloat16),
            pltpu.VMEM((2, W, VOX * COLS), jnp.bfloat16),
            pltpu.SemaphoreType.DMA((PARTS,)),
            pltpu.SemaphoreType.DMA((2,)),
        ],
        compiler_params=pltpu.CompilerParams(vmem_limit_bytes=VMEM_LIMIT),
        cost_estimate=pl.CostEstimate(flops=10**10, bytes_accessed=10**7, transcendentals=0),
    )(where, stacked, *pieces)


def moved(a, dy, dh, dc):
    perm = []
    for v in range(VOX):
        y, h, c = v // 4, (v // 2) % 2, v % 2
        perm.append((((y + dy) % 4) * 4 + (h ^ dh) * 2 + (c ^ dc), v))
    return lax.ppermute(a, "vox", perm)


PLACES = [(dy, dh, dc) for dy in range(4) for dh in range(2) for dc in range(2)]
PIECES = 13


def part_list(n):
    h = n // 2
    whole = [(1, 0), (3, 0), (0, 1)]
    split = [[(1, 1), 0, (2, 0), 0], [(3, 1), 0, (2, 0), h], [(1, 1), h, (3, 1), h]]
    listed = []
    for dc in range(2):
        at = [PLACES.index(k + (dc,)) for k in whole]
        listed.append((9 * dc, 0, PLACES.index((0, 0, dc)), 0, n))
        for e in range(3):
            listed.append((1 + e, 0, at[e], 0, n) if dc == 0 else (10, e * n, at[e], 0, n))
        for e, (first, low, second, high) in enumerate(split):
            ref, off = (4 + e, 0) if dc == 0 else (11, e * n)
            listed.append((ref, off, PLACES.index(first + (dc,)), low, h))
            listed.append((ref, off + h, PLACES.index(second + (dc,)), high, h))
        last = PLACES.index((2, 1, dc))
        listed.append((7, 0, last, 0, h) if dc == 0 else (12, 0, last, 0, h))
        listed.append((8, 0, last, h, h) if dc == 0 else (12, h, last, h, h))
    return listed


ROW_PARTS = part_list(STEP * SUBJ // 2)
DUAL_PARTS = part_list(COLS)
PARTS = len(ROW_PARTS)


def gather_parts(own):
    half = own.shape[0] // 2
    up, down, side = moved(own, 1, 0, 0), moved(own, 3, 0, 0), moved(own, 0, 1, 0)
    twin = moved(own, 0, 0, 1)
    join = functools.partial(jnp.concatenate, axis=0)
    from_up = moved(join([side[:half], up[:half]]), 1, 0, 0)
    from_down = moved(join([side[:half], down[half:]]), 3, 0, 0)
    from_side = moved(join([up[half:], down[half:]]), 0, 1, 0)
    far_up, far_down = moved(from_up[:half], 1, 0, 0), moved(from_side[half:], 3, 0, 0)
    twin_first = moved(join([up, down, side]), 0, 0, 1)
    twin_second = moved(join([from_up, from_down, from_side]), 0, 0, 1)
    twin_third = moved(join([far_up, far_down]), 0, 0, 1)
    return [own, up, down, side, from_up, from_down, from_side, far_up, far_down] + [
        twin, twin_first, twin_second, twin_third,
    ]


def lanczos(ticks, centers):
    distance = ticks[None, :] - centers[:, None]
    inside = jnp.abs(distance) < 3 * TICKS
    scaled = distance.astype(jnp.float32) / TICKS
    shaped = jnp.sinc(scaled) * jnp.sinc(scaled / 3.0)
    return jnp.where(inside, shaped, jnp.zeros_like(shaped)).astype(jnp.bfloat16)


def all_offsets(offsets, group):
    row = lax.broadcasted_iota(jnp.int32, (SUBJ, 128), 0)
    table = jnp.where(row == group, offsets[0], 0)
    table = table + lax.ppermute(table, "subj", [(i, i ^ 1) for i in range(SUBJ)])
    rest = [lax.ppermute(table, "subj", [(i, i ^ hop) for i in range(SUBJ)]) for hop in (2, 4, 6)]
    return (table + rest[0] + rest[1] + rest[2])[:, 0]


def body(features, token_ticks, offsets, run_lengths, penalty, responses):
    group = lax.axis_index("subj")
    vox = lax.axis_index("vox")
    core = vox % 2
    chip = group * CHIPS + vox // 2
    left, right = features[:, :HALF], features[:, HALF:]
    mine = jnp.where(core == 0, left, right)
    theirs = lax.ppermute(jnp.where(core == 0, right, left), "vox", [(i, i ^ 1) for i in range(VOX)])
    every = all_offsets(offsets + (theirs[0, 0] * 0).astype(jnp.int32), group)
    first = jnp.where(core == 0, mine, theirs)
    second = jnp.where(core == 0, theirs, mine)
    count = SUBJ * VOX
    before = lax.ppermute(second[-HALO:], ("subj", "vox"), [(i, i + 2) for i in range(count - 2)])
    after = lax.ppermute(first[:HALO], ("subj", "vox"), [(i + 2, i) for i in range(count - 2)])
    ext = jnp.concatenate([before, first, second, after], axis=0)
    far = jnp.full((HALO,), -(2**20), jnp.int32)
    span = ext.shape[0]
    near_ticks = lax.dynamic_slice_in_dim(
        jnp.concatenate([far, token_ticks, far]), chip * (span - 2 * HALO), span, 0
    )
    spread = (GAP / TICKS) ** 0.5
    steps = chip * STEP + jnp.arange(STEP, dtype=jnp.int32)
    centers = (steps[None, :] * TICKS + every[:, None]).reshape(-1)
    table = lanczos(near_ticks, centers)
    summed = jnp.dot(table, ext, preferred_element_type=jnp.float32)
    local = (summed * spread).astype(jnp.bfloat16).reshape(SUBJ, STEP, HALF)
    rows = lax.all_to_all(local, "subj", split_axis=0, concat_axis=0, tiled=True).reshape(SUBJ * STEP, HALF)
    cutrow = SUBJ * STEP // 2
    pieces = gather_parts(rows[:cutrow])
    gathered = lax.all_gather(rows[cutrow:] + sum(p[:1, :1] for p in pieces[1:4]) * 0, "vox", axis=0, tiled=False)

    lengths = run_lengths[0]
    starts = jnp.cumsum(lengths) - lengths
    tr_steps = jnp.arange(N, dtype=jnp.int32)
    run_first = jnp.max(jnp.where(starts[None, :] <= tr_steps[:, None], starts[None, :], 0), axis=1)
    pos = tr_steps - run_first
    row_pos, col_pos = pos[:, None], jnp.broadcast_to(pos[None, :], (8, N))
    y, h = vox // 4, (vox // 2) % 2
    where = jnp.stack([((y + dy) % 4) * 4 + (h ^ dh) * 2 + (core ^ dc) for dy, dh, dc in PLACES])
    *state, slab_first = first_call(where, penalty, pieces, responses[0].T, row_pos, col_pos)
    dual, slab_second = second_call(where, penalty, gathered, state, row_pos, col_pos)
    interp = jnp.concatenate([slab_first, slab_second], axis=0)
    delayed = []
    for k in range(1, DELAYS + 1):
        shifted = jnp.concatenate([jnp.zeros((k, SLAB), interp.dtype), interp[:-k]], axis=0)
        delayed.append(jnp.where((pos >= k)[:, None], shifted, jnp.zeros_like(shifted)))
    stacked = jnp.concatenate(delayed, axis=1).T
    projected = project_call(where, stacked, gather_parts(dual))
    return projected.reshape(1, DELAYS, SLAB, projected.shape[1])


def solution(mesh):
    return jax.shard_map(
        body,
        mesh=mesh,
        in_specs=(
            P(("subj", "vox"), None),
            P(),
            P("subj"),
            P("subj", None),
            P("subj"),
            P("subj", None, "vox"),
        ),
        out_specs=P("subj", None, "vox", None),
        check_vma=False,
    )
```

```python
import functools

import jax
import jax.numpy as jnp
from jax import lax
from jax.experimental import pallas as pl
from jax.experimental.pallas import tpu as pltpu
from jax.sharding import PartitionSpec as P

DELAYS = 4
TICKS = 64
GAP = 6
F = 4096
SUBJ = 8
VOX = 16
N = 1536
SLAB = F // VOX
COLS = 128
W = 256
PANELS = N // W
EDGE = 16
HALO = 32
VMEM_LIMIT = 52 * 2**20
STEP = 24
HALF = F // 2
CHIPS = 8
PART = N // 2
CUTP = PANELS // 2
HI = lax.Precision.HIGHEST
NT = (((1,), (1,)), ((), ()))


def mm(a, b):
    return jnp.dot(a, b, precision=HI, preferred_element_type=jnp.float32)


def mmt(a, b):
    return lax.dot_general(a, b, NT, precision=HI, preferred_element_type=jnp.float32)


def tree(terms):
    while len(terms) > 1:
        terms = [terms[i] + terms[i + 1] for i in range(0, len(terms), 2)]
    return terms[0]


def tri_inverse(block):
    rows = [block[8 * g : 8 * g + 8, :] for g in range(16)]
    shape = (8, 128)
    lane = lax.broadcasted_iota(jnp.int32, shape, 1)
    sub = lax.broadcasted_iota(jnp.int32, shape, 0)
    zero = jnp.where(lane + sub >= 1000, 1.0, 0.0)
    spot = [jnp.where(sub == p, 1.0, 0.0) for p in range(8)]
    none = jnp.zeros(shape, jnp.float32)

    def across(v, c):
        return jnp.broadcast_to(v[:, c : c + 1], shape)

    def down(v, r):
        return jnp.broadcast_to(v[r : r + 1, :], shape)

    def inside(low, high):
        return (lane >= low) & (lane < high)

    def pivots(row, base, col, extra):
        u = jnp.where(inside(base, base + 8), jnp.where(lane - base == sub, 1.0, 0.0), row)
        out = u
        for p in range(8):
            pivot = down(col[p], p)
            root, inv = lax.rsqrt(pivot), 1.0 / pivot
            h = col[p] - spot[p]
            top = down(u, p)
            out = jnp.where(sub == p, top * root, out)
            u = u - (h * top) * inv
            for m in range(p + 1, 8):
                col[m] = col[m] - (h * down(col[m], p)) * inv
            for m in range(len(extra)):
                extra[m] = extra[m] - (h * down(extra[m], p)) * inv
        return u, out

    def minus(row, low, high, factors, full):
        return jnp.where(inside(low, high), 0.0, row) - tree([f * v for f, v in zip(factors, full)])

    far = None
    for g in range(0, 16, 2):
        base = 8 * g
        first, second = rows[g], rows[g + 1]
        col = [across(first, base + m) + zero for m in range(8)]
        side = [across(second, base + q) for q in range(8)]
        if far is not None:
            ids, low, left, right = far
            later = mm(left, right)
        ahead = [across(first, base + 8 + m) + zero for m in range(8)]
        diag = [across(second, base + 8 + m) for m in range(8)]
        u, out = pivots(first, base, col, ahead)
        rows[g] = jnp.where(lane < base + 8, out, 0.0)
        col = [diag[m] - tree([side[q] * down(ahead[m], q) for q in range(8)]) for m in range(8)]
        second = minus(second, base, base + 8, side, [down(u, q) for q in range(8)])
        cross = [across(u, base + 8 + q) for q in range(8)]
        v, out = pivots(second, base + 8, col, [])
        rows[g + 1] = jnp.where(lane < base + 16, out, 0.0)
        if far is not None:
            for n, i in enumerate(ids):
                rows[i] = jnp.where(inside(low, low + 16), 0.0, rows[i]) - later[8 * n : 8 * n + 8]
            far = None
        if g == 14:
            break
        u = minus(u, base + 8, base + 16, cross, [down(v, q) for q in range(8)])
        full = [down(u, q) for q in range(8)] + [down(v, q) for q in range(8)]
        ids = list(range(g + 4, 16))
        if ids:
            left = jnp.concatenate([rows[i] for i in ids], axis=0)
            right = jnp.concatenate([none] * g + [u, v] + [none] * (14 - g), axis=0)
            far = (ids, base, left, right)
        for i in (g + 2, g + 3):
            factors = [across(rows[i], base + q) for q in range(16)]
            rows[i] = minus(rows[i], base, base + 16, factors, full)
    return jnp.concatenate(rows, axis=0)


def cut(i, size=W):
    return pl.ds(pl.multiple_of(i * size, size), size)


def assemble(raw_ref, xs_ref, first):
    for g in range(SUBJ // 2):
        low = STEP * g // 16 * 16
        off = STEP * g - low

        def one(u, _, g=g, low=low, off=off):
            dest = pl.ds(pl.multiple_of(first + 192 * g + 48 * u, 16), 48)
            for c in range(2):
                pair = [
                    raw_ref[4 * u + 2 * e + c, low : low + 32, :].astype(jnp.float32)[off : off + STEP]
                    for e in range(2)
                ]
                xs_ref[dest, c * HALF : (c + 1) * HALF] = jnp.concatenate(pair, axis=0).astype(jnp.bfloat16)
            return 0

        lax.fori_loop(0, CHIPS // 2, one, 0)


def gram_rows(first, last, pen, xs_ref, a_ref, strip_ref, turn_ref, pr_ref, pc_ref):
    scale = 1.0 / (DELAYS * F)

    def gram(i, _):
        left = xs_ref[pl.ds(pl.multiple_of(i * W, W), W + EDGE), :]

        def one(j):
            right = xs_ref[pl.ds(pl.multiple_of(j * W + EDGE, EDGE), W), :]
            strip_ref[:, pl.ds(pl.multiple_of(j * W + 128, 128), W)] = lax.dot_general(
                left, right, NT, preferred_element_type=jnp.float32
            )

        row_pos = jnp.broadcast_to(pr_ref[cut(i), :], (W, 128))
        lane = lax.broadcasted_iota(jnp.int32, (W + EDGE, 128), 1)

        def shift(j):
            at = [pl.ds(pl.multiple_of(j * W + 128 * e, 128), 128) for e in range(3)]
            for e in range(2):
                back, here = strip_ref[:, at[e]], strip_ref[:, at[e + 1]]
                for k in range(1, DELAYS + 1):
                    turn_ref[k - 1, e] = pltpu.roll(jnp.where(lane >= 128 - k, back, here), k, 1)
            for e in range(2):
                near = jnp.minimum(row_pos, pc_ref[0:1, at[e]])
                parts = [
                    jnp.where(near >= k, turn_ref[k - 1, e, EDGE - k : EDGE - k + W, :], 0.0)
                    for k in range(1, DELAYS + 1)
                ]
                a_ref[cut(i), at[e]] = tree(parts) * scale

        def both(j, _):
            shift(j - 1)
            one(j)
            return 0

        one(0)
        lax.fori_loop(1, i + 1, both, 0)
        shift(i)
        row = lax.broadcasted_iota(jnp.int32, (W, W), 0)
        column = lax.broadcasted_iota(jnp.int32, (W, W), 1)
        a_ref[cut(i), cut(i)] += jnp.where(row == column, pen, 0.0)
        return 0

    lax.fori_loop(first, last, gram, 0)


def diagonal(p, a_ref, inv_ref):
    top, below = cut(2 * p, 128), cut(2 * p + 1, 128)
    first = tri_inverse(a_ref[top, top])
    c = mmt(a_ref[below, top], first)
    turned = mm(c, first)
    second = tri_inverse(a_ref[below, below] - mmt(c, c))
    inv_ref[p, 0:128, 0:128] = first
    inv_ref[p, 128:256, 128:256] = second
    inv_ref[p, 128:256, 0:128] = -mm(second, turned)
    inv_ref[p, 0:128, 128:256] = jnp.zeros((128, 128), jnp.float32)


def eliminate(p, first, last, a_ref, inv_ref):
    here = cut(p)

    def scale_rows(i, _):
        a_ref[cut(i), here] = mmt(a_ref[cut(i), here], inv_ref[p])
        return 0

    lax.fori_loop(first, last, scale_rows, 0)

    def column(j, _):
        right = a_ref[cut(j), here]

        def update(i, _):
            a_ref[cut(i), cut(j)] -= mmt(a_ref[cut(i), here], right)
            return 0

        lax.fori_loop(jnp.maximum(j, first), last, update, 0)
        return 0

    lax.fori_loop(p + 1, last, column, 0)


def forward(p, first, last, a_ref, inv_ref, tail_ref):
    here = cut(p)

    def update(j, _):
        tail_ref[:, cut(j)] -= mmt(tail_ref[:, here], a_ref[cut(j), here])
        return 0

    lax.fori_loop(first, last, update, 0)


def first_kernel(*refs):
    (where_ref, pen_ref), refs = refs[:2], refs[2:]
    pieces, refs = refs[:PIECES], refs[PIECES:]
    b_ref, pr_ref, pc_ref, rows_out, low_out, inv_out, tail_out, slab_out = refs[:8]
    raw_ref, xs_ref, a_ref, strip_ref, turn_ref, inv_ref, tail_ref, sem = refs[8:]
    copies = []
    for n, (ref, off, key, start, size) in enumerate(ROW_PARTS):
        source = pieces[ref].at[pl.ds(off, size), :]
        copies.append(pltpu.make_async_copy(source, raw_ref.at[where_ref[key], pl.ds(start, size), :], sem.at[n]))
    copies.append(pltpu.make_async_copy(b_ref, tail_ref, sem.at[PARTS]))
    for c in copies:
        c.start()
    xs_ref[0:EDGE, :] = jnp.zeros((EDGE, F), jnp.bfloat16)
    strip_ref[:, 0:128] = jnp.zeros((W + EDGE, 128), jnp.float32)
    for c in copies:
        c.wait()
    assemble(raw_ref, xs_ref, EDGE)
    own = pl.ds(EDGE, PART)
    mine = pl.ds(pl.multiple_of(where_ref[0] * SLAB, SLAB), SLAB)
    outs = [
        pltpu.make_async_copy(xs_ref.at[own, :], rows_out, sem.at[PARTS + 1]),
        pltpu.make_async_copy(xs_ref.at[own, mine], slab_out, sem.at[PARTS + 2]),
    ]
    for c in outs:
        c.start()
    gram_rows(0, CUTP, pen_ref[0], xs_ref, a_ref, strip_ref, turn_ref, pr_ref, pc_ref)

    def panel(p, _):
        diagonal(p, a_ref, inv_ref)
        eliminate(p, p + 1, CUTP, a_ref, inv_ref)
        tail_ref[:, cut(p)] = mmt(tail_ref[:, cut(p)], inv_ref[p])
        forward(p, p + 1, CUTP, a_ref, inv_ref, tail_ref)
        return 0

    lax.fori_loop(0, CUTP, panel, 0)
    more = [
        pltpu.make_async_copy(a_ref, low_out, sem.at[PARTS + 3]),
        pltpu.make_async_copy(inv_ref, inv_out, sem.at[PARTS + 4]),
        pltpu.make_async_copy(tail_ref, tail_out, sem.at[PARTS + 5]),
    ]
    for c in more:
        c.start()
    for c in outs + more:
        c.wait()


def second_kernel(
    where_ref, pen_ref, all_ref, rows_in, low_in, inv_in, tail_in, pr_ref, pc_ref, o_ref, slab_out,
    raw_ref, xs_ref, a_ref, strip_ref, turn_ref, inv_ref, tail_ref, sem,
):
    chunk = pltpu.make_async_copy(all_ref, raw_ref, sem.at[0])
    copies = [
        pltpu.make_async_copy(rows_in, xs_ref.at[pl.ds(EDGE, PART), :], sem.at[1]),
        pltpu.make_async_copy(low_in, a_ref.at[pl.ds(0, PART), pl.ds(0, PART)], sem.at[2]),
        pltpu.make_async_copy(inv_in, inv_ref.at[pl.ds(0, CUTP)], sem.at[3]),
        pltpu.make_async_copy(tail_in, tail_ref, sem.at[4]),
    ]
    chunk.start()
    for c in copies:
        c.start()
    strip_ref[:, 0:128] = jnp.zeros((W + EDGE, 128), jnp.float32)
    chunk.wait()
    assemble(raw_ref, xs_ref, EDGE + PART)
    mine = pl.ds(pl.multiple_of(where_ref[0] * SLAB, SLAB), SLAB)
    slab = pltpu.make_async_copy(xs_ref.at[pl.ds(EDGE + PART, PART), mine], slab_out, sem.at[5])
    slab.start()
    for c in copies:
        c.wait()
    gram_rows(CUTP, PANELS, pen_ref[0], xs_ref, a_ref, strip_ref, turn_ref, pr_ref, pc_ref)

    for p in range(CUTP):
        here = slice(p * W, (p + 1) * W)
        new = mmt(a_ref[PART:N, here], inv_ref[p])
        a_ref[PART:N, here] = new
        for j in range(p + 1, PANELS):
            there = slice(j * W, (j + 1) * W)
            top = max(j * W - PART, 0)
            right = a_ref[there, here] if j < CUTP else new[top : top + W]
            a_ref[PART + top : N, there] -= mmt(new[top:], right)
        tail_ref[:, PART:N] -= mmt(tail_ref[:, here], new)

    def panel(p, _):
        diagonal(p, a_ref, inv_ref)
        eliminate(p, p + 1, PANELS, a_ref, inv_ref)
        tail_ref[:, cut(p)] = mmt(tail_ref[:, cut(p)], inv_ref[p])
        forward(p, p + 1, PANELS, a_ref, inv_ref, tail_ref)
        return 0

    lax.fori_loop(CUTP, PANELS, panel, 0)

    for p in reversed(range(PANELS)):
        here = slice(p * W, (p + 1) * W)
        x = mm(tail_ref[:, here], inv_ref[p])
        tail_ref[:, here] = x
        if p:
            tail_ref[:, : p * W] -= mm(x, a_ref[here, : p * W])
    o_ref[...] = tail_ref[...].astype(o_ref.dtype)
    slab.wait()


ANYWHERE = pl.BlockSpec(memory_space=pl.ANY)
IN_VMEM = pl.BlockSpec(memory_space=pltpu.VMEM)
IN_SMEM = pl.BlockSpec(memory_space=pltpu.SMEM)


def scratches(rows, sems):
    return [
        pltpu.VMEM((VOX, STEP * SUBJ // 2, HALF), jnp.bfloat16),
        pltpu.VMEM((rows + EDGE, F), jnp.bfloat16),
        pltpu.VMEM((rows, rows), jnp.float32),
        pltpu.VMEM((W + EDGE, rows + 128), jnp.float32),
        pltpu.VMEM((DELAYS, 2, W + EDGE, 128), jnp.float32),
        pltpu.VMEM((rows // W, W, W), jnp.float32),
        pltpu.VMEM((COLS, N), jnp.float32),
        pltpu.SemaphoreType.DMA((sems,)),
    ]


def first_call(where, pen, pieces, targets, row_pos, col_pos):
    return pl.pallas_call(
        first_kernel,
        out_shape=[
            jax.ShapeDtypeStruct((PART, F), jnp.bfloat16),
            jax.ShapeDtypeStruct((PART, PART), jnp.float32),
            jax.ShapeDtypeStruct((CUTP, W, W), jnp.float32),
            jax.ShapeDtypeStruct((COLS, N), jnp.float32),
            jax.ShapeDtypeStruct((PART, SLAB), jnp.bfloat16),
        ],
        in_specs=[IN_SMEM, IN_SMEM] + [ANYWHERE] * PIECES + [ANYWHERE, IN_VMEM, IN_VMEM],
        out_specs=[ANYWHERE] * 5,
        scratch_shapes=scratches(PART, PARTS + 6),
        compiler_params=pltpu.CompilerParams(vmem_limit_bytes=VMEM_LIMIT),
        cost_estimate=pl.CostEstimate(flops=3 * 10**10, bytes_accessed=2 * 10**7, transcendentals=0),
    )(where, pen, *pieces, targets, row_pos, col_pos)


def second_call(where, pen, gathered, state, row_pos, col_pos):
    return pl.pallas_call(
        second_kernel,
        out_shape=[
            jax.ShapeDtypeStruct((COLS, N), jnp.bfloat16),
            jax.ShapeDtypeStruct((PART, SLAB), jnp.bfloat16),
        ],
        in_specs=[IN_SMEM, IN_SMEM] + [ANYWHERE] * 5 + [IN_VMEM, IN_VMEM],
        out_specs=[IN_VMEM, ANYWHERE],
        scratch_shapes=scratches(N, 6),
        compiler_params=pltpu.CompilerParams(vmem_limit_bytes=VMEM_LIMIT),
        cost_estimate=pl.CostEstimate(flops=5 * 10**10, bytes_accessed=2 * 10**7, transcendentals=0),
    )(where, pen, gathered, *state, row_pos, col_pos)


def fetch_parts(where_ref, pieces, listed, xt_ref, sem):
    chips = {}
    for n, (ref, off, key, start, size) in enumerate(listed):
        row = pl.multiple_of(where_ref[key] * COLS + start, 16)
        source = pieces[ref].at[pl.ds(off, size), :]
        copy = pltpu.make_async_copy(source, xt_ref.at[pl.ds(row, size), :], sem.at[n])
        copy.start()
        chips.setdefault(key // 2, []).append(copy)
    return chips


def chip_columns(where_ref, chip):
    return pl.ds(pl.multiple_of(where_ref[2 * chip] // 2 * W, W), W)


def project(st, xt):
    got = lax.dot_general(st, xt, NT, preferred_element_type=jnp.float32)
    return (got * (DELAYS * F) ** (-0.5)).astype(jnp.bfloat16)


def near_kernel(where_ref, st_ref, *refs):
    pieces, (out_ref, xt_ref, buf_ref, sem, out_sem) = refs[: len(NEAR)], refs[len(NEAR) :]
    chips = fetch_parts(where_ref, dict(zip(NEAR, pieces)), NEAR_PARTS, xt_ref, sem)
    sent = []
    for n, chip in enumerate(chips):
        slot = n % 2
        for c in chips[chip]:
            c.wait()
        if n >= 2:
            sent[n - 2].wait()
        buf_ref[slot] = project(st_ref[...], xt_ref[chip_columns(where_ref, chip), :])
        sent.append(pltpu.make_async_copy(buf_ref.at[slot], out_ref.at[n], out_sem.at[slot]))
        sent[n].start()
    for c in sent[-2:]:
        c.wait()


def rest_kernel(where_ref, st_ref, begun_ref, *refs):
    pieces, (out_ref, xt_ref, buf_ref, sem, begun_sem, out_sem) = refs[: len(REST)], refs[len(REST) :]
    chips = fetch_parts(where_ref, dict(zip(REST, pieces)), REST_PARTS, xt_ref, sem)
    near = list(dict.fromkeys(item[2] // 2 for item in NEAR_PARTS))
    blocks = buf_ref.shape[0]
    size = buf_ref.shape[1]
    begun = []
    for n in range(blocks):
        for k, chip in enumerate(near):
            source = begun_ref.at[k, pl.ds(n * size, size), :]
            target = buf_ref.at[n, :, chip_columns(where_ref, chip)]
            begun.append(pltpu.make_async_copy(source, target, begun_sem.at[n, k]))
            begun[-1].start()
    sent = []
    for n in range(blocks):
        rows = slice(n * size, (n + 1) * size)
        for chip in chips:
            if n == 0:
                for c in chips[chip]:
                    c.wait()
            at = chip_columns(where_ref, chip)
            buf_ref[n, :, at] = project(st_ref[rows, :], xt_ref[at, :])
        for c in begun[n * len(near) : (n + 1) * len(near)]:
            c.wait()
        sent.append(pltpu.make_async_copy(buf_ref.at[n], out_ref.at[rows, :], out_sem.at[n]))
        sent[n].start()
    for c in sent:
        c.wait()


def near_call(where, stacked, pieces):
    return pl.pallas_call(
        near_kernel,
        out_shape=jax.ShapeDtypeStruct((VOX // 4, DELAYS * SLAB, W), jnp.bfloat16),
        in_specs=[IN_SMEM, IN_VMEM] + [ANYWHERE] * len(NEAR),
        out_specs=ANYWHERE,
        scratch_shapes=[
            pltpu.VMEM((VOX * COLS, N), jnp.bfloat16),
            pltpu.VMEM((2, DELAYS * SLAB, W), jnp.bfloat16),
            pltpu.SemaphoreType.DMA((len(NEAR_PARTS),)),
            pltpu.SemaphoreType.DMA((2,)),
        ],
        compiler_params=pltpu.CompilerParams(vmem_limit_bytes=VMEM_LIMIT),
        cost_estimate=pl.CostEstimate(flops=5 * 10**9, bytes_accessed=8 * 10**6, transcendentals=0),
    )(where, stacked, *pieces)


def rest_call(where, stacked, begun, pieces):
    return pl.pallas_call(
        rest_kernel,
        out_shape=jax.ShapeDtypeStruct((DELAYS * SLAB, VOX * COLS), jnp.bfloat16),
        in_specs=[IN_SMEM, IN_VMEM] + [ANYWHERE] * (1 + len(REST)),
        out_specs=ANYWHERE,
        scratch_shapes=[
            pltpu.VMEM((VOX * COLS, N), jnp.bfloat16),
            pltpu.VMEM((2, DELAYS * SLAB // 2, VOX * COLS), jnp.bfloat16),
            pltpu.SemaphoreType.DMA((len(REST_PARTS),)),
            pltpu.SemaphoreType.DMA((2, VOX // 4)),
            pltpu.SemaphoreType.DMA((2,)),
        ],
        compiler_params=pltpu.CompilerParams(vmem_limit_bytes=VMEM_LIMIT),
        cost_estimate=pl.CostEstimate(flops=5 * 10**9, bytes_accessed=12 * 10**6, transcendentals=0),
    )(where, stacked, begun, *pieces)


def moved(a, dy, dh, dc):
    perm = []
    for v in range(VOX):
        y, h, c = v // 4, (v // 2) % 2, v % 2
        perm.append((((y + dy) % 4) * 4 + (h ^ dh) * 2 + (c ^ dc), v))
    return lax.ppermute(a, "vox", perm)


PLACES = [(dy, dh, dc) for dy in range(4) for dh in range(2) for dc in range(2)]
PIECES = 13


def part_list(n):
    h = n // 2
    whole = [(1, 0), (3, 0), (0, 1)]
    split = [[(1, 1), 0, (2, 0), 0], [(3, 1), 0, (2, 0), h], [(1, 1), h, (3, 1), h]]
    listed = []
    for dc in range(2):
        at = [PLACES.index(k + (dc,)) for k in whole]
        listed.append((9 * dc, 0, PLACES.index((0, 0, dc)), 0, n))
        for e in range(3):
            listed.append((1 + e, 0, at[e], 0, n) if dc == 0 else (10, e * n, at[e], 0, n))
        for e, (first, low, second, high) in enumerate(split):
            ref, off = (4 + e, 0) if dc == 0 else (11, e * n)
            listed.append((ref, off, PLACES.index(first + (dc,)), low, h))
            listed.append((ref, off + h, PLACES.index(second + (dc,)), high, h))
        last = PLACES.index((2, 1, dc))
        listed.append((7, 0, last, 0, h) if dc == 0 else (12, 0, last, 0, h))
        listed.append((8, 0, last, h, h) if dc == 0 else (12, h, last, h, h))
    return listed


ROW_PARTS = part_list(STEP * SUBJ // 2)
DUAL_PARTS = part_list(COLS)
PARTS = len(ROW_PARTS)
NEAR = [0, 1, 2, 3, 9, 10]
REST = [4, 5, 6, 7, 8, 11, 12]
NEAR_PARTS = sorted((item for item in DUAL_PARTS if item[0] in NEAR), key=lambda item: item[2] // 2)
REST_PARTS = sorted((item for item in DUAL_PARTS if item[0] in REST), key=lambda item: item[2] // 2)


def gather_parts(own, between=None):
    half = own.shape[0] // 2
    up, down, side = moved(own, 1, 0, 0), moved(own, 3, 0, 0), moved(own, 0, 1, 0)
    twin = moved(own, 0, 0, 1)
    join = functools.partial(jnp.concatenate, axis=0)
    from_up = moved(join([side[:half], up[:half]]), 1, 0, 0)
    from_down = moved(join([side[:half], down[half:]]), 3, 0, 0)
    from_side = moved(join([up[half:], down[half:]]), 0, 1, 0)
    twin_first = moved(join([up, down, side]), 0, 0, 1)
    low, high, second = from_up[:half], from_side[half:], join([from_up, from_down, from_side])
    begun = None
    if between is not None:
        begun = between([own, up, down, side, twin, twin_first])
        hold = begun[0, :1, :1] * 0
        low, high, second = low + hold, high + hold, second + hold
    far_up, far_down = moved(low, 1, 0, 0), moved(high, 3, 0, 0)
    twin_second = moved(second, 0, 0, 1)
    twin_third = moved(join([far_up, far_down]), 0, 0, 1)
    return [own, up, down, side, from_up, from_down, from_side, far_up, far_down] + [
        twin, twin_first, twin_second, twin_third,
    ], begun


def lanczos(ticks, centers):
    distance = ticks[None, :] - centers[:, None]
    inside = jnp.abs(distance) < 3 * TICKS
    scaled = distance.astype(jnp.float32) / TICKS
    shaped = jnp.sinc(scaled) * jnp.sinc(scaled / 3.0)
    return jnp.where(inside, shaped, jnp.zeros_like(shaped)).astype(jnp.bfloat16)


def all_offsets(offsets, group, hold):
    row = lax.broadcasted_iota(jnp.int32, (SUBJ, 128), 0)
    table = jnp.where(row == group, offsets[0], 0)
    table = table + lax.ppermute(table, "subj", [(i, i ^ 1) for i in range(SUBJ)])
    table = table + hold
    rest = [lax.ppermute(table, "subj", [(i, i ^ hop) for i in range(SUBJ)]) for hop in (2, 4, 6)]
    return (table + rest[0] + rest[1] + rest[2])[:, 0]


def body(features, token_ticks, offsets, run_lengths, penalty, responses):
    group = lax.axis_index("subj")
    vox = lax.axis_index("vox")
    core = vox % 2
    chip = group * CHIPS + vox // 2
    left, right = features[:, :HALF], features[:, HALF:]
    mine = jnp.where(core == 0, left, right)
    theirs = lax.ppermute(jnp.where(core == 0, right, left), "vox", [(i, i ^ 1) for i in range(VOX)])
    every = all_offsets(offsets, group, (theirs[0, 0] * 0).astype(jnp.int32))
    first = jnp.where(core == 0, mine, theirs)
    second = jnp.where(core == 0, theirs, mine)
    count = SUBJ * VOX
    before = lax.ppermute(second[-HALO:], ("subj", "vox"), [(i, i + 2) for i in range(count - 2)])
    after = lax.ppermute(first[:HALO], ("subj", "vox"), [(i + 2, i) for i in range(count - 2)])
    ext = jnp.concatenate([before, first, second, after], axis=0)
    far = jnp.full((HALO,), -(2**20), jnp.int32)
    span = ext.shape[0]
    near_ticks = lax.dynamic_slice_in_dim(
        jnp.concatenate([far, token_ticks, far]), chip * (span - 2 * HALO), span, 0
    )
    spread = (GAP / TICKS) ** 0.5
    steps = chip * STEP + jnp.arange(STEP, dtype=jnp.int32)
    centers = (steps[None, :] * TICKS + every[:, None]).reshape(-1)
    table = lanczos(near_ticks, centers)
    summed = jnp.dot(table, ext, preferred_element_type=jnp.float32)
    local = (summed * spread).astype(jnp.bfloat16).reshape(SUBJ, STEP, HALF)
    rows = lax.all_to_all(local, "subj", split_axis=0, concat_axis=0, tiled=True).reshape(SUBJ * STEP, HALF)
    cutrow = SUBJ * STEP // 2
    pieces, _ = gather_parts(rows[:cutrow])
    gathered = lax.all_gather(rows[cutrow:] + sum(p[:1, :1] for p in pieces[1:4]) * 0, "vox", axis=0, tiled=False)

    lengths = run_lengths[0]
    starts = jnp.cumsum(lengths) - lengths
    tr_steps = jnp.arange(N, dtype=jnp.int32)
    run_first = jnp.max(jnp.where(starts[None, :] <= tr_steps[:, None], starts[None, :], 0), axis=1)
    pos = tr_steps - run_first
    row_pos, col_pos = pos[:, None], jnp.broadcast_to(pos[None, :], (8, N))
    y, h = vox // 4, (vox // 2) % 2
    where = jnp.stack([((y + dy) % 4) * 4 + (h ^ dh) * 2 + (core ^ dc) for dy, dh, dc in PLACES])
    *state, slab_first = first_call(where, penalty, pieces, responses[0].T, row_pos, col_pos)
    dual, slab_second = second_call(where, penalty, gathered, state, row_pos, col_pos)
    interp = jnp.concatenate([slab_first, slab_second], axis=0)
    delayed = []
    for k in range(1, DELAYS + 1):
        shifted = jnp.concatenate([jnp.zeros((k, SLAB), interp.dtype), interp[:-k]], axis=0)
        delayed.append(jnp.where((pos >= k)[:, None], shifted, jnp.zeros_like(shifted)))
    stacked = jnp.concatenate(delayed, axis=1).T
    parts, begun = gather_parts(dual, functools.partial(near_call, where, stacked))
    projected = rest_call(where, stacked, begun, [parts[n] for n in REST])
    return projected.reshape(1, DELAYS, SLAB, projected.shape[1])


def solution(mesh):
    return jax.shard_map(
        body,
        mesh=mesh,
        in_specs=(
            P(("subj", "vox"), None),
            P(),
            P("subj"),
            P("subj", None),
            P("subj"),
            P("subj", None, "vox"),
        ),
        out_specs=P("subj", None, "vox", None),
        check_vma=False,
    )
```

```python
import functools

import jax
import jax.numpy as jnp
from jax import lax
from jax.experimental import pallas as pl
from jax.experimental.pallas import tpu as pltpu
from jax.sharding import PartitionSpec as P

DELAYS = 4
TICKS = 64
GAP = 6
F = 4096
SUBJ = 8
VOX = 16
N = 1536
SLAB = F // VOX
COLS = 128
W = 256
PANELS = N // W
EDGE = 16
HALO = 32
VMEM_LIMIT = 52 * 2**20
STEP = 24
HALF = F // 2
CHIPS = 8
PART = N // 2
CUTP = PANELS // 2
HI = lax.Precision.HIGHEST
NT = (((1,), (1,)), ((), ()))


def mm(a, b):
    return jnp.dot(a, b, precision=HI, preferred_element_type=jnp.float32)


def mmt(a, b):
    return lax.dot_general(a, b, NT, precision=HI, preferred_element_type=jnp.float32)


def tree(terms):
    while len(terms) > 1:
        terms = [terms[i] + terms[i + 1] for i in range(0, len(terms), 2)]
    return terms[0]


def tri_inverse(block):
    rows = [block[8 * g : 8 * g + 8, :] for g in range(16)]
    shape = (8, 128)
    lane = lax.broadcasted_iota(jnp.int32, shape, 1)
    sub = lax.broadcasted_iota(jnp.int32, shape, 0)
    zero = jnp.where(lane + sub >= 1000, 1.0, 0.0)
    spot = [jnp.where(sub == p, 1.0, 0.0) for p in range(8)]
    none = jnp.zeros(shape, jnp.float32)

    def across(v, c):
        return jnp.broadcast_to(v[:, c : c + 1], shape)

    def down(v, r):
        return jnp.broadcast_to(v[r : r + 1, :], shape)

    def inside(low, high):
        return (lane >= low) & (lane < high)

    def pivots(row, base, col, extra):
        u = jnp.where(inside(base, base + 8), jnp.where(lane - base == sub, 1.0, 0.0), row)
        out = u
        for p in range(8):
            pivot = down(col[p], p)
            root, inv = lax.rsqrt(pivot), 1.0 / pivot
            h = col[p] - spot[p]
            top = down(u, p)
            out = jnp.where(sub == p, top * root, out)
            u = u - (h * top) * inv
            for m in range(p + 1, 8):
                col[m] = col[m] - (h * down(col[m], p)) * inv
            for m in range(len(extra)):
                extra[m] = extra[m] - (h * down(extra[m], p)) * inv
        return u, out

    def minus(row, low, high, factors, full):
        return jnp.where(inside(low, high), 0.0, row) - tree([f * v for f, v in zip(factors, full)])

    far = None
    for g in range(0, 16, 2):
        base = 8 * g
        first, second = rows[g], rows[g + 1]
        col = [across(first, base + m) + zero for m in range(8)]
        side = [across(second, base + q) for q in range(8)]
        if far is not None:
            ids, low, left, right = far
            later = mm(left, right)
        ahead = [across(first, base + 8 + m) + zero for m in range(8)]
        diag = [across(second, base + 8 + m) for m in range(8)]
        u, out = pivots(first, base, col, ahead)
        rows[g] = jnp.where(lane < base + 8, out, 0.0)
        col = [diag[m] - tree([side[q] * down(ahead[m], q) for q in range(8)]) for m in range(8)]
        second = minus(second, base, base + 8, side, [down(u, q) for q in range(8)])
        cross = [across(u, base + 8 + q) for q in range(8)]
        v, out = pivots(second, base + 8, col, [])
        rows[g + 1] = jnp.where(lane < base + 16, out, 0.0)
        if far is not None:
            for n, i in enumerate(ids):
                rows[i] = jnp.where(inside(low, low + 16), 0.0, rows[i]) - later[8 * n : 8 * n + 8]
            far = None
        if g == 14:
            break
        u = minus(u, base + 8, base + 16, cross, [down(v, q) for q in range(8)])
        full = [down(u, q) for q in range(8)] + [down(v, q) for q in range(8)]
        ids = list(range(g + 4, 16))
        if ids:
            left = jnp.concatenate([rows[i] for i in ids], axis=0)
            right = jnp.concatenate([none] * g + [u, v] + [none] * (14 - g), axis=0)
            far = (ids, base, left, right)
        for i in (g + 2, g + 3):
            factors = [across(rows[i], base + q) for q in range(16)]
            rows[i] = minus(rows[i], base, base + 16, factors, full)
    return jnp.concatenate(rows, axis=0)


def cut(i, size=W):
    return pl.ds(pl.multiple_of(i * size, size), size)


def assemble(raw_ref, xs_ref, first):
    for g in range(SUBJ // 2):
        low = STEP * g // 16 * 16
        off = STEP * g - low

        def one(u, _, g=g, low=low, off=off):
            dest = pl.ds(pl.multiple_of(first + 192 * g + 48 * u, 16), 48)
            for c in range(2):
                pair = [
                    raw_ref[4 * u + 2 * e + c, low : low + 32, :].astype(jnp.float32)[off : off + STEP]
                    for e in range(2)
                ]
                xs_ref[dest, c * HALF : (c + 1) * HALF] = jnp.concatenate(pair, axis=0).astype(jnp.bfloat16)
            return 0

        lax.fori_loop(0, CHIPS // 2, one, 0)


def gram_rows(first, last, pen, xs_ref, a_ref, strip_ref, turn_ref, pr_ref, pc_ref):
    scale = 1.0 / (DELAYS * F)

    def gram(i, _):
        left = xs_ref[pl.ds(pl.multiple_of(i * W, W), W + EDGE), :]

        def one(j):
            right = xs_ref[pl.ds(pl.multiple_of(j * W + EDGE, EDGE), W), :]
            strip_ref[:, pl.ds(pl.multiple_of(j * W + 128, 128), W)] = lax.dot_general(
                left, right, NT, preferred_element_type=jnp.float32
            )

        row_pos = jnp.broadcast_to(pr_ref[cut(i), :], (W, 128))
        lane = lax.broadcasted_iota(jnp.int32, (W + EDGE, 128), 1)

        def shift(j):
            at = [pl.ds(pl.multiple_of(j * W + 128 * e, 128), 128) for e in range(3)]
            for e in range(2):
                back, here = strip_ref[:, at[e]], strip_ref[:, at[e + 1]]
                for k in range(1, DELAYS + 1):
                    turn_ref[k - 1, e] = pltpu.roll(jnp.where(lane >= 128 - k, back, here), k, 1)
            for e in range(2):
                near = jnp.minimum(row_pos, pc_ref[0:1, at[e]])
                parts = [
                    jnp.where(near >= k, turn_ref[k - 1, e, EDGE - k : EDGE - k + W, :], 0.0)
                    for k in range(1, DELAYS + 1)
                ]
                a_ref[cut(i), at[e]] = tree(parts) * scale

        def both(j, _):
            shift(j - 1)
            one(j)
            return 0

        one(0)
        lax.fori_loop(1, i + 1, both, 0)
        shift(i)
        row = lax.broadcasted_iota(jnp.int32, (W, W), 0)
        column = lax.broadcasted_iota(jnp.int32, (W, W), 1)
        a_ref[cut(i), cut(i)] += jnp.where(row == column, pen, 0.0)
        return 0

    lax.fori_loop(first, last, gram, 0)


def diagonal(p, a_ref, inv_ref):
    top, below = cut(2 * p, 128), cut(2 * p + 1, 128)
    first = tri_inverse(a_ref[top, top])
    c = mmt(a_ref[below, top], first)
    turned = mm(c, first)
    second = tri_inverse(a_ref[below, below] - mmt(c, c))
    inv_ref[p, 0:128, 0:128] = first
    inv_ref[p, 128:256, 128:256] = second
    inv_ref[p, 128:256, 0:128] = -mm(second, turned)
    inv_ref[p, 0:128, 128:256] = jnp.zeros((128, 128), jnp.float32)


def eliminate(p, first, last, a_ref, inv_ref):
    here = cut(p)

    def scale_rows(i, _):
        a_ref[cut(i), here] = mmt(a_ref[cut(i), here], inv_ref[p])
        return 0

    lax.fori_loop(first, last, scale_rows, 0)

    def column(j, _):
        right = a_ref[cut(j), here]

        def update(i, _):
            a_ref[cut(i), cut(j)] -= mmt(a_ref[cut(i), here], right)
            return 0

        lax.fori_loop(jnp.maximum(j, first), last, update, 0)
        return 0

    lax.fori_loop(p + 1, last, column, 0)


def forward(p, first, last, a_ref, inv_ref, tail_ref):
    here = cut(p)

    def update(j, _):
        tail_ref[:, cut(j)] -= mmt(tail_ref[:, here], a_ref[cut(j), here])
        return 0

    lax.fori_loop(first, last, update, 0)


def first_kernel(*refs):
    (where_ref, pen_ref), refs = refs[:2], refs[2:]
    pieces, refs = refs[:PIECES], refs[PIECES:]
    b_ref, pr_ref, pc_ref, rows_out, low_out, inv_out, tail_out, slab_out = refs[:8]
    raw_ref, xs_ref, a_ref, strip_ref, turn_ref, inv_ref, tail_ref, sem = refs[8:]
    copies = []
    for n, (ref, off, key, start, size) in enumerate(ROW_PARTS):
        source = pieces[ref].at[pl.ds(off, size), :]
        copies.append(pltpu.make_async_copy(source, raw_ref.at[where_ref[key], pl.ds(start, size), :], sem.at[n]))
    copies.append(pltpu.make_async_copy(b_ref, tail_ref, sem.at[PARTS]))
    for c in copies:
        c.start()
    xs_ref[0:EDGE, :] = jnp.zeros((EDGE, F), jnp.bfloat16)
    strip_ref[:, 0:128] = jnp.zeros((W + EDGE, 128), jnp.float32)
    for c in copies:
        c.wait()
    assemble(raw_ref, xs_ref, EDGE)
    own = pl.ds(EDGE, PART)
    mine = pl.ds(pl.multiple_of(where_ref[0] * SLAB, SLAB), SLAB)
    outs = [
        pltpu.make_async_copy(xs_ref.at[own, :], rows_out, sem.at[PARTS + 1]),
        pltpu.make_async_copy(xs_ref.at[own, mine], slab_out, sem.at[PARTS + 2]),
    ]
    for c in outs:
        c.start()
    gram_rows(0, CUTP, pen_ref[0], xs_ref, a_ref, strip_ref, turn_ref, pr_ref, pc_ref)

    def panel(p, _):
        diagonal(p, a_ref, inv_ref)
        eliminate(p, p + 1, CUTP, a_ref, inv_ref)
        tail_ref[:, cut(p)] = mmt(tail_ref[:, cut(p)], inv_ref[p])
        forward(p, p + 1, CUTP, a_ref, inv_ref, tail_ref)
        return 0

    lax.fori_loop(0, CUTP, panel, 0)
    more = [
        pltpu.make_async_copy(a_ref, low_out, sem.at[PARTS + 3]),
        pltpu.make_async_copy(inv_ref, inv_out, sem.at[PARTS + 4]),
        pltpu.make_async_copy(tail_ref, tail_out, sem.at[PARTS + 5]),
    ]
    for c in more:
        c.start()
    for c in outs + more:
        c.wait()


def second_kernel(
    where_ref, pen_ref, all_ref, rows_in, low_in, inv_in, tail_in, pr_ref, pc_ref, o_ref, slab_out,
    raw_ref, xs_ref, a_ref, strip_ref, turn_ref, inv_ref, tail_ref, sem,
):
    chunk = pltpu.make_async_copy(all_ref, raw_ref, sem.at[0])
    copies = [
        pltpu.make_async_copy(rows_in, xs_ref.at[pl.ds(EDGE, PART), :], sem.at[1]),
        pltpu.make_async_copy(low_in, a_ref.at[pl.ds(0, PART), pl.ds(0, PART)], sem.at[2]),
        pltpu.make_async_copy(inv_in, inv_ref.at[pl.ds(0, CUTP)], sem.at[3]),
        pltpu.make_async_copy(tail_in, tail_ref, sem.at[4]),
    ]
    chunk.start()
    for c in copies:
        c.start()
    strip_ref[:, 0:128] = jnp.zeros((W + EDGE, 128), jnp.float32)
    chunk.wait()
    assemble(raw_ref, xs_ref, EDGE + PART)
    mine = pl.ds(pl.multiple_of(where_ref[0] * SLAB, SLAB), SLAB)
    slab = pltpu.make_async_copy(xs_ref.at[pl.ds(EDGE + PART, PART), mine], slab_out, sem.at[5])
    slab.start()
    for c in copies:
        c.wait()
    gram_rows(CUTP, PANELS, pen_ref[0], xs_ref, a_ref, strip_ref, turn_ref, pr_ref, pc_ref)

    for p in range(CUTP):
        here = slice(p * W, (p + 1) * W)
        new = mmt(a_ref[PART:N, here], inv_ref[p])
        a_ref[PART:N, here] = new
        for j in range(p + 1, PANELS):
            there = slice(j * W, (j + 1) * W)
            top = max(j * W - PART, 0)
            right = a_ref[there, here] if j < CUTP else new[top : top + W]
            a_ref[PART + top : N, there] -= mmt(new[top:], right)
        tail_ref[:, PART:N] -= mmt(tail_ref[:, here], new)

    def panel(p, _):
        diagonal(p, a_ref, inv_ref)
        eliminate(p, p + 1, PANELS, a_ref, inv_ref)
        tail_ref[:, cut(p)] = mmt(tail_ref[:, cut(p)], inv_ref[p])
        forward(p, p + 1, PANELS, a_ref, inv_ref, tail_ref)
        return 0

    lax.fori_loop(CUTP, PANELS, panel, 0)

    for p in reversed(range(PANELS)):
        here = slice(p * W, (p + 1) * W)
        x = mm(tail_ref[:, here], inv_ref[p])
        tail_ref[:, here] = x
        if p:
            tail_ref[:, : p * W] -= mm(x, a_ref[here, : p * W])
    o_ref[...] = tail_ref[...].astype(o_ref.dtype)
    slab.wait()


ANYWHERE = pl.BlockSpec(memory_space=pl.ANY)
IN_VMEM = pl.BlockSpec(memory_space=pltpu.VMEM)
IN_SMEM = pl.BlockSpec(memory_space=pltpu.SMEM)


def scratches(rows, sems):
    return [
        pltpu.VMEM((VOX, STEP * SUBJ // 2, HALF), jnp.bfloat16),
        pltpu.VMEM((rows + EDGE, F), jnp.bfloat16),
        pltpu.VMEM((rows, rows), jnp.float32),
        pltpu.VMEM((W + EDGE, rows + 128), jnp.float32),
        pltpu.VMEM((DELAYS, 2, W + EDGE, 128), jnp.float32),
        pltpu.VMEM((rows // W, W, W), jnp.float32),
        pltpu.VMEM((COLS, N), jnp.float32),
        pltpu.SemaphoreType.DMA((sems,)),
    ]


def first_call(where, pen, pieces, targets, row_pos, col_pos):
    return pl.pallas_call(
        first_kernel,
        out_shape=[
            jax.ShapeDtypeStruct((PART, F), jnp.bfloat16),
            jax.ShapeDtypeStruct((PART, PART), jnp.float32),
            jax.ShapeDtypeStruct((CUTP, W, W), jnp.float32),
            jax.ShapeDtypeStruct((COLS, N), jnp.float32),
            jax.ShapeDtypeStruct((PART, SLAB), jnp.bfloat16),
        ],
        in_specs=[IN_SMEM, IN_SMEM] + [ANYWHERE] * PIECES + [ANYWHERE, IN_VMEM, IN_VMEM],
        out_specs=[ANYWHERE] * 5,
        scratch_shapes=scratches(PART, PARTS + 6),
        compiler_params=pltpu.CompilerParams(vmem_limit_bytes=VMEM_LIMIT),
        cost_estimate=pl.CostEstimate(flops=3 * 10**10, bytes_accessed=2 * 10**7, transcendentals=0),
    )(where, pen, *pieces, targets, row_pos, col_pos)


def second_call(where, pen, gathered, state, row_pos, col_pos):
    return pl.pallas_call(
        second_kernel,
        out_shape=[
            jax.ShapeDtypeStruct((COLS, N), jnp.bfloat16),
            jax.ShapeDtypeStruct((PART, SLAB), jnp.bfloat16),
        ],
        in_specs=[IN_SMEM, IN_SMEM] + [ANYWHERE] * 5 + [IN_VMEM, IN_VMEM],
        out_specs=[IN_VMEM, ANYWHERE],
        scratch_shapes=scratches(N, 6),
        compiler_params=pltpu.CompilerParams(vmem_limit_bytes=VMEM_LIMIT),
        cost_estimate=pl.CostEstimate(flops=5 * 10**10, bytes_accessed=2 * 10**7, transcendentals=0),
    )(where, pen, gathered, *state, row_pos, col_pos)


def fetch_parts(where_ref, pieces, listed, xt_ref, sem):
    chips = {}
    for n, (ref, off, key, start, size) in enumerate(listed):
        row = pl.multiple_of(where_ref[key] * COLS + start, 16)
        source = pieces[ref].at[pl.ds(off, size), :]
        copy = pltpu.make_async_copy(source, xt_ref.at[pl.ds(row, size), :], sem.at[n])
        copy.start()
        chips.setdefault(key // 2, []).append(copy)
    return chips


def chip_columns(where_ref, chip):
    return pl.ds(pl.multiple_of(where_ref[2 * chip] // 2 * W, W), W)


def project(st, xt):
    got = lax.dot_general(st, xt, NT, preferred_element_type=jnp.float32)
    return (got * (DELAYS * F) ** (-0.5)).astype(jnp.bfloat16)


def project_kernel(where_ref, st_ref, *refs):
    pieces, (out_ref, xt_ref, buf_ref, sem, out_sem) = refs[:PIECES], refs[PIECES:]
    listed = sorted(DUAL_PARTS, key=lambda item: item[2] // 2)
    chips = fetch_parts(where_ref, pieces, listed, xt_ref, sem)
    sent = []
    for n, chip in enumerate(chips):
        for c in chips[chip]:
            c.wait()
        at = chip_columns(where_ref, chip)
        if n < len(chips) - 1:
            buf_ref[:, at] = project(st_ref[...], xt_ref[at, :])
            continue
        for r in range(DELAYS):
            rows = slice(r * SLAB, (r + 1) * SLAB)
            buf_ref[rows, at] = project(st_ref[rows, :], xt_ref[at, :])
            sent.append(pltpu.make_async_copy(buf_ref.at[rows, :], out_ref.at[rows, :], out_sem.at[r]))
            sent[r].start()
    for c in sent:
        c.wait()


def project_call(where, stacked, pieces):
    return pl.pallas_call(
        project_kernel,
        out_shape=jax.ShapeDtypeStruct((DELAYS * SLAB, VOX * COLS), jnp.bfloat16),
        in_specs=[IN_SMEM, IN_VMEM] + [ANYWHERE] * PIECES,
        out_specs=ANYWHERE,
        scratch_shapes=[
            pltpu.VMEM((VOX * COLS, N), jnp.bfloat16),
            pltpu.VMEM((DELAYS * SLAB, VOX * COLS), jnp.bfloat16),
            pltpu.SemaphoreType.DMA((PARTS,)),
            pltpu.SemaphoreType.DMA((DELAYS,)),
        ],
        compiler_params=pltpu.CompilerParams(vmem_limit_bytes=VMEM_LIMIT),
        cost_estimate=pl.CostEstimate(flops=10**10, bytes_accessed=10**7, transcendentals=0),
    )(where, stacked, *pieces)


def moved(a, dy, dh, dc):
    perm = []
    for v in range(VOX):
        y, h, c = v // 4, (v // 2) % 2, v % 2
        perm.append((((y + dy) % 4) * 4 + (h ^ dh) * 2 + (c ^ dc), v))
    return lax.ppermute(a, "vox", perm)


PLACES = [(dy, dh, dc) for dy in range(4) for dh in range(2) for dc in range(2)]
PIECES = 13


def part_list(n):
    h = n // 2
    whole = [(1, 0), (3, 0), (0, 1)]
    split = [[(1, 1), 0, (2, 0), 0], [(3, 1), 0, (2, 0), h], [(1, 1), h, (3, 1), h]]
    listed = []
    for dc in range(2):
        at = [PLACES.index(k + (dc,)) for k in whole]
        listed.append((9 * dc, 0, PLACES.index((0, 0, dc)), 0, n))
        for e in range(3):
            listed.append((1 + e, 0, at[e], 0, n) if dc == 0 else (10, e * n, at[e], 0, n))
        for e, (first, low, second, high) in enumerate(split):
            ref, off = (4 + e, 0) if dc == 0 else (11, e * n)
            listed.append((ref, off, PLACES.index(first + (dc,)), low, h))
            listed.append((ref, off + h, PLACES.index(second + (dc,)), high, h))
        last = PLACES.index((2, 1, dc))
        listed.append((7, 0, last, 0, h) if dc == 0 else (12, 0, last, 0, h))
        listed.append((8, 0, last, h, h) if dc == 0 else (12, h, last, h, h))
    return listed


ROW_PARTS = part_list(STEP * SUBJ // 2)
DUAL_PARTS = part_list(COLS)
PARTS = len(ROW_PARTS)


def gather_parts(own):
    half = own.shape[0] // 2
    up, down, side = moved(own, 1, 0, 0), moved(own, 3, 0, 0), moved(own, 0, 1, 0)
    twin = moved(own, 0, 0, 1)
    join = functools.partial(jnp.concatenate, axis=0)
    from_up = moved(join([side[:half], up[:half]]), 1, 0, 0)
    from_down = moved(join([side[:half], down[half:]]), 3, 0, 0)
    from_side = moved(join([up[half:], down[half:]]), 0, 1, 0)
    far_up, far_down = moved(from_up[:half], 1, 0, 0), moved(from_side[half:], 3, 0, 0)
    twin_first = moved(join([up, down, side]), 0, 0, 1)
    twin_second = moved(join([from_up, from_down, from_side]), 0, 0, 1)
    twin_third = moved(join([far_up, far_down]), 0, 0, 1)
    return [own, up, down, side, from_up, from_down, from_side, far_up, far_down] + [
        twin, twin_first, twin_second, twin_third,
    ]


def lanczos(ticks, centers):
    distance = ticks[None, :] - centers[:, None]
    inside = jnp.abs(distance) < 3 * TICKS
    scaled = distance.astype(jnp.float32) / TICKS
    shaped = jnp.sinc(scaled) * jnp.sinc(scaled / 3.0)
    return jnp.where(inside, shaped, jnp.zeros_like(shaped)).astype(jnp.bfloat16)


def all_offsets(offsets, group, hold):
    row = lax.broadcasted_iota(jnp.int32, (SUBJ, 128), 0)
    table = jnp.where(row == group, offsets[0], 0)
    table = table + lax.ppermute(table, "subj", [(i, i ^ 1) for i in range(SUBJ)])
    table = table + hold
    rest = [lax.ppermute(table, "subj", [(i, i ^ hop) for i in range(SUBJ)]) for hop in (2, 4, 6)]
    return (table + rest[0] + rest[1] + rest[2])[:, 0]


def body(features, token_ticks, offsets, run_lengths, penalty, responses):
    group = lax.axis_index("subj")
    vox = lax.axis_index("vox")
    core = vox % 2
    chip = group * CHIPS + vox // 2
    left, right = features[:, :HALF], features[:, HALF:]
    mine = jnp.where(core == 0, left, right)
    theirs = lax.ppermute(jnp.where(core == 0, right, left), "vox", [(i, i ^ 1) for i in range(VOX)])
    every = all_offsets(offsets, group, (theirs[0, 0] * 0).astype(jnp.int32))
    first = jnp.where(core == 0, mine, theirs)
    second = jnp.where(core == 0, theirs, mine)
    count = SUBJ * VOX
    before = lax.ppermute(second[-HALO:], ("subj", "vox"), [(i, i + 2) for i in range(count - 2)])
    after = lax.ppermute(first[:HALO], ("subj", "vox"), [(i + 2, i) for i in range(count - 2)])
    ext = jnp.concatenate([before, first, second, after], axis=0)
    far = jnp.full((HALO,), -(2**20), jnp.int32)
    span = ext.shape[0]
    near_ticks = lax.dynamic_slice_in_dim(
        jnp.concatenate([far, token_ticks, far]), chip * (span - 2 * HALO), span, 0
    )
    spread = (GAP / TICKS) ** 0.5
    steps = chip * STEP + jnp.arange(STEP, dtype=jnp.int32)
    centers = (steps[None, :] * TICKS + every[:, None]).reshape(-1)
    table = lanczos(near_ticks, centers)
    summed = jnp.dot(table, ext, preferred_element_type=jnp.float32)
    local = (summed * spread).astype(jnp.bfloat16).reshape(SUBJ, STEP, HALF)
    rows = lax.all_to_all(local, "subj", split_axis=0, concat_axis=0, tiled=True).reshape(SUBJ * STEP, HALF)
    cutrow = SUBJ * STEP // 2
    pieces = gather_parts(rows[:cutrow])
    gathered = lax.all_gather(rows[cutrow:] + sum(p[:1, :1] for p in pieces[1:4]) * 0, "vox", axis=0, tiled=False)

    lengths = run_lengths[0]
    starts = jnp.cumsum(lengths) - lengths
    tr_steps = jnp.arange(N, dtype=jnp.int32)
    run_first = jnp.max(jnp.where(starts[None, :] <= tr_steps[:, None], starts[None, :], 0), axis=1)
    pos = tr_steps - run_first
    row_pos, col_pos = pos[:, None], jnp.broadcast_to(pos[None, :], (8, N))
    y, h = vox // 4, (vox // 2) % 2
    where = jnp.stack([((y + dy) % 4) * 4 + (h ^ dh) * 2 + (core ^ dc) for dy, dh, dc in PLACES])
    *state, slab_first = first_call(where, penalty, pieces, responses[0].T, row_pos, col_pos)
    dual, slab_second = second_call(where, penalty, gathered, state, row_pos, col_pos)
    interp = jnp.concatenate([slab_first, slab_second], axis=0)
    delayed = []
    for k in range(1, DELAYS + 1):
        shifted = jnp.concatenate([jnp.zeros((k, SLAB), interp.dtype), interp[:-k]], axis=0)
        delayed.append(jnp.where((pos >= k)[:, None], shifted, jnp.zeros_like(shifted)))
    stacked = jnp.concatenate(delayed, axis=1).T
    projected = project_call(where, stacked, gather_parts(dual))
    return projected.reshape(1, DELAYS, SLAB, projected.shape[1])


def solution(mesh):
    return jax.shard_map(
        body,
        mesh=mesh,
        in_specs=(
            P(("subj", "vox"), None),
            P(),
            P("subj"),
            P("subj", None),
            P("subj"),
            P("subj", None, "vox"),
        ),
        out_specs=P("subj", None, "vox", None),
        check_vma=False,
    )
```
